128 devices in a mesh: dp: 8 (over x, core), expert: 16 (over y, z).
Axes of the slice: x: 4, y: 4, z: 4, core: 2. Of those that a mesh axis runs over, the one named last changes fastest.
Arguments:
- grad_parts: bfloat16 [8, 128, 512, 512], P('dp', 'expert'), may hold values from -6 to 6
- stat_owned: float32 [16, 16, 512, 512], P('expert', 'dp'), as said below
- owner_list: int32 [128], replicated, may hold values from 0 to 15, as said below
Outputs:
- new_stat: float32 [16, 16, 512, 512], P('expert', 'dp')
- precond: float32 [128, 512, 512], P('expert', 'dp')
The draws below stay inside these ranges and needn't reach their ends.
Inputs may be any that keep to these rules, and one draw needn't show every extreme that they name: `owner_list`: blocks e * 8 to e * 8 + 7 come from expert shard e and go to 8 different owners; some owner holds a block from every one of the 16 shards. `stat_owned`: every slot is symmetric and strictly diagonally dominant with a positive diagonal.
All inputs are finite; a program needn't handle non-finite values.
Results may differ from the reference program's by a relative error of at most 0.0003.
Values may be sent and summed in bfloat16 or wider, within the bound.
A program may use at most 128 MiB of HBM per device.

```python
import math
import jax
import jax.numpy as jnp
from jax import lax

B = 512
ITERS = 6
BPS = 8
NB = 128
N_DP = 8
N_EXPERT = 16


def draw_stat_owned(key, part):
    key = jax.random.fold_in(key, 5)
    key_diag, key_off = jax.random.split(key, 2)
    lowest, highest = (1.0, 10.0)
    levels = jnp.exp(jax.random.uniform(key_diag, (N_EXPERT, N_EXPERT, B), jnp.float32, math.log(lowest), math.log(highest)))
    noise_field = jax.random.uniform(key_off, (N_EXPERT, N_EXPERT, B, B), jnp.float32, -1.0, 1.0)
    mixed = noise_field
    mixed = 0.5 * (mixed + jnp.swapaxes(mixed, -1, -2))
    limits = jnp.minimum(levels[..., :, None], levels[..., None, :])
    identity = jnp.eye(B, dtype=jnp.float32)
    return (1.0 - identity) * (0.95 / B) * mixed * limits + identity * levels[..., None]


def draw_owner_list(key, part):
    key = jax.random.fold_in(key, 11)
    key_heavy, key_favour, key_noise, key_order = jax.random.split(key, 4)
    owners = jnp.arange(N_EXPERT, dtype=jnp.int32)
    heavy_owner = jax.random.randint(key_heavy, (), 0, N_EXPERT, dtype=jnp.int32)
    favour = jax.random.randint(key_favour, (N_EXPERT,), 0, 4, dtype=jnp.int32)
    noise_field = jax.random.randint(key_noise, (N_EXPERT, N_EXPERT), 0, 8, dtype=jnp.int32)
    scores = (noise_field + 3 * favour[None, :]) * N_EXPERT + owners[None, :]
    scores = jnp.where(owners[None, :] == heavy_owner, 1000 * N_EXPERT, scores)
    chosen = lax.top_k(scores, BPS)[1].astype(jnp.int32)
    shuffles = jax.random.split(key_order, N_EXPERT)
    chosen = jax.vmap(jax.random.permutation)(shuffles, chosen)
    return chosen.reshape(N_EXPERT * BPS).astype(jnp.int32)


def shard_levels(key, shape, pieces, smallest, largest):
    def one(position, shards_of):
        heights = jax.random.uniform(jax.random.fold_in(jax.random.fold_in(key, 6), position), (shards_of,), jnp.float32, smallest / len(pieces), largest / len(pieces))
        return jnp.repeat(jnp.exp(heights), shape[position] // shards_of).reshape((-1,) + (1,) * (len(shape) - position - 1))

    gain = one(*pieces[0])
    for cut in pieces[1:]:
        gain = gain * one(*cut)
    return gain


def centred(key, extent, scale, reach, pieces=(), held_as=jnp.bfloat16):
    loudness = shard_levels(key, extent, pieces, -0.22, 0.18) if pieces else 1.0
    values = jax.random.normal(key, extent, jnp.float32) * scale * loudness
    return jnp.minimum(jnp.maximum(values, -reach), reach).astype(held_as)


def setup_inputs(seed: int = 0) -> dict:
    streams_of = jax.random.split(jax.random.key(seed), 4)
    grad_parts = centred(streams_of[0], (N_DP, NB, B, B), 0.7, 6.0, ((0, 8), (1, 16)))
    stat_owned = draw_stat_owned(jax.random.fold_in(streams_of[3], 71), 0)
    owner_list = draw_owner_list(jax.random.fold_in(streams_of[3], 71), 0)
    return dict(grad_parts=grad_parts, stat_owned=stat_owned, owner_list=owner_list)


EPSILON = 1e-06
DECAY = 0.9
GAIN = 0.1

def product(former, latter):
    return jnp.dot(former, latter, precision=lax.Precision.HIGHEST, preferred_element_type=jnp.float32)

def inverse_root(matrix):
    identity = jnp.eye(matrix.shape[-1], dtype=jnp.float32)
    damped = matrix + EPSILON * identity
    scaling = 5.0 / (2.0 * jnp.sqrt(jnp.sum(damped * damped)))
    current = scaling * damped
    result = jnp.power(scaling, 0.25) * identity
    for repeat in range(ITERS):
        factor = 1.25 * identity - 0.25 * current
        square = product(factor, factor)
        current = product(product(square, square), current)
        result = product(result, factor)
    return result

def reference(grad_parts, stat_owned, owner_list):
    summed = lax.optimization_barrier(jnp.sum(grad_parts.astype(jnp.float32), axis=0))
    sources = (jnp.arange(NB) // BPS).astype(jnp.int32)
    outer_terms = lax.map(lambda grad_block: product(grad_block, grad_block.T), summed)
    slot_terms = jnp.zeros(stat_owned.shape, jnp.float32).at[owner_list, sources].set(outer_terms)
    new_stat = DECAY * stat_owned + GAIN / B * slot_terms
    picked = new_stat[owner_list, sources]

    def refresh_block(paired):
        return product(inverse_root(paired[0]), paired[1])
    precond = lax.map(refresh_block, (picked, summed))
    return (new_stat, precond)
```

```python
import functools

import jax
import jax.numpy as jnp
from jax import lax
from jax.experimental import pallas as pl
from jax.experimental.pallas import tpu as pltpu
from jax.sharding import PartitionSpec as P

ITERS = 6
EPSILON = 1e-06
DECAY = 0.9
GAIN = 0.1

MESH = pl.DeviceIdType.MESH
F32 = jnp.float32
BF16 = jnp.bfloat16
TILE = 128
RING = 4
CORES = 2


def remote(src, dst, send_sem, recv_sem, dp, expert):
    return pltpu.make_async_remote_copy(
        src_ref=src,
        dst_ref=dst,
        send_sem=send_sem,
        recv_sem=recv_sem,
        device_id={"dp": dp, "expert": expert},
        device_id_type=MESH,
    )


def split(value):
    high = value.astype(BF16)
    return high, (value - high.astype(F32)).astype(BF16)


def dot(former, latter):
    return jnp.dot(former, latter, preferred_element_type=F32)


def dot_transposed(former, latter):
    return lax.dot_general(former, latter, (((1,), (1,)), ((), ())), preferred_element_type=F32)


def diagonal(rows, first, columns):
    across = lax.broadcasted_iota(jnp.int32, (rows, columns), 1)
    return lax.broadcasted_iota(jnp.int32, (rows, columns), 0) + first == across


class Pair:
    def __init__(self, refs):
        self.high, self.low = refs

    def put(self, rows, value):
        self.high[rows, :], self.low[rows, :] = split(value)


def product(former, latter, rows):
    return dot(former.high[rows, :], latter.high[...]) + (
        dot(former.high[rows, :], latter.low[...]) + dot(former.low[rows, :], latter.high[...])
    )


def kernel(
    extent,
    blocks,
    experts,
    owner_ref,
    grads,
    stats,
    fresh_out,
    precond_out,
    own,
    part,
    far_sum,
    right_sum,
    left_sum,
    total,
    rx_far,
    rx_direct,
    rx_mixed,
    previous,
    packed,
    gathered,
    chosen,
    home_stat,
    term,
    terms_in,
    terms_out,
    owner_terms,
    matrix,
    halves,
    updates,
    load_sem,
    stat_sem,
    core_send,
    core_recv,
    ring_send,
    ring_recv,
    plane_send,
    plane_recv,
    home_send,
    home_recv,
    back_send,
    back_recv,
    spread_send,
    spread_recv,
    band_send,
    band_recv,
    out_sem,
):
    dp = lax.axis_index("dp")
    spot = lax.axis_index("expert")
    x, core = dp // CORES, dp % CORES
    twin = x * CORES + 1 - core
    right = lax.rem(x + 1, RING) * CORES + core
    left = lax.rem(x + RING - 1, RING) * CORES + core
    slot, band = lax.rem(spot, 2), spot // 2
    served = 2 * dp + slot
    own_band = band == dp
    tiles = extent // TILE
    upper = [(a, b) for a in range(tiles) for b in range(a, tiles)]
    depth = len(upper) * TILE // blocks
    half = extent // 2

    def block_of(turn, which):
        return lax.rem(x + turn, RING) * CORES + which

    loads = {}
    for turn in (2, 1, 3, 0):
        loads[turn] = pltpu.make_async_copy(
            grads.at[block_of(turn, core)], own.at[turn], load_sem.at[turn]
        )
        loads[turn].start()
    stat_load = pltpu.make_async_copy(stats, previous, stat_sem)
    stat_load.start()

    barrier = pltpu.get_barrier_semaphore()

    def greet(to_dp, to_expert):
        pl.semaphore_signal(
            barrier, inc=1, device_id={"dp": to_dp, "expert": to_expert}, device_id_type=MESH
        )

    @pl.loop(1, experts)
    def _(step):
        greet(dp, lax.rem(spot + step, experts))

    @pl.loop(1, blocks)
    def _(step):
        greet(lax.rem(dp + step, blocks), spot)

    @pl.loop(0, blocks)
    def _(step):
        @pl.when(jnp.logical_not(jnp.logical_and(own_band, step == dp)))
        def _():
            greet(step, served)
            greet(band, 2 * step + slot)

    pl.semaphore_wait(barrier, experts - 1 + blocks - 1 + 2 * blocks - jnp.where(own_band, 2, 0))

    crossing = {}
    for turn in (2, 1, 3, 0):
        crossing[turn] = remote(
            grads.at[block_of(turn, 1 - core)],
            part.at[turn],
            core_send.at[turn],
            core_recv.at[turn],
            twin,
            spot,
        )
        crossing[turn].start()

    def pair_sum(turn, rows):
        return own[turn, rows, :].astype(F32) + part[turn, rows, :].astype(F32)

    top, bottom = pl.ds(0, half), pl.ds(half, half)

    def ring(index, src, dst, to):
        return remote(src, dst, ring_send.at[index], ring_recv.at[index], to, spot)

    loads[2].wait()
    crossing[2].wait_recv()
    far_sum[top, :] = pair_sum(2, top)
    far_right = ring(0, far_sum.at[top], rx_far.at[0], right)
    far_right.start()
    far_sum[bottom, :] = pair_sum(2, bottom)
    far_left = ring(1, far_sum.at[bottom], rx_far.at[1], left)
    far_left.start()

    loads[1].wait()
    crossing[1].wait_recv()
    right_sum[bottom, :] = pair_sum(1, bottom)
    direct_right = ring(2, right_sum.at[bottom], rx_direct.at[1], right)
    direct_right.start()
    loads[3].wait()
    crossing[3].wait_recv()
    left_sum[top, :] = pair_sum(3, top)
    direct_left = ring(3, left_sum.at[top], rx_direct.at[0], left)
    direct_left.start()

    stat_load.wait()
    for where in range(2):
        for place, (a, b) in enumerate(upper):
            packed[where, place * TILE : (place + 1) * TILE, :] = previous[
                where, a * TILE : (a + 1) * TILE, b * TILE : (b + 1) * TILE
            ]

    def rows_of(index):
        return pl.ds(pl.multiple_of(index * depth, depth), depth)

    def to_plane(other):
        return remote(
            packed.at[lax.rem(other, 2), rows_of(other // 2)],
            gathered.at[spot],
            plane_send.at[other],
            plane_recv.at[spot],
            dp,
            other,
        )

    def from_plane(other):
        return remote(
            packed.at[0, rows_of(0)], gathered.at[other], plane_send.at[other], plane_recv.at[other], dp, other
        )

    @pl.loop(1, experts)
    def _(step):
        to_plane(lax.rem(spot + step, experts)).start()

    gathered[spot] = packed[slot, rows_of(band), :]

    right_sum[top, :] = pair_sum(1, top)
    left_sum[bottom, :] = pair_sum(3, bottom)
    loads[0].wait()
    crossing[0].wait_recv()
    total[...] = pair_sum(0, pl.ds(0, extent))

    far_right.wait_recv()
    right_sum[top, :] = right_sum[top, :] + rx_far[0]
    mixed_right = ring(4, right_sum.at[top], rx_mixed.at[0], right)
    mixed_right.start()
    far_left.wait_recv()
    left_sum[bottom, :] = left_sum[bottom, :] + rx_far[1]
    mixed_left = ring(5, left_sum.at[bottom], rx_mixed.at[1], left)
    mixed_left.start()

    @pl.loop(1, experts)
    def _(step):
        from_plane(lax.rem(spot + step, experts)).wait_recv()

    def to_home(index):
        return remote(
            chosen.at[index],
            home_stat.at[rows_of(band)],
            home_send.at[index],
            home_recv.at[band],
            index,
            served,
        )

    def from_home(index):
        return remote(
            chosen.at[index],
            home_stat.at[rows_of(index)],
            home_send.at[index],
            home_recv.at[index],
            band,
            2 * index + slot,
        )

    for index in range(blocks):
        chosen[index] = gathered[owner_ref[served * blocks + index]]

    @pl.loop(0, blocks)
    def _(index):
        mine = jnp.logical_and(own_band, index == dp)

        @pl.when(jnp.logical_not(mine))
        def _():
            to_home(index).start()

        @pl.when(mine)
        def _():
            home_stat[rows_of(index), :] = chosen[index]

    direct_left.wait_recv()
    total[top, :] = total[top, :] + rx_direct[0]
    direct_right.wait_recv()
    total[bottom, :] = total[bottom, :] + rx_direct[1]
    mixed_right.wait_recv()
    total[top, :] = total[top, :] + rx_mixed[0]
    mixed_left.wait_recv()
    total[bottom, :] = total[bottom, :] + rx_mixed[1]

    grad, current, factor, result, square = (
        Pair((halves.at[2 * index], halves.at[2 * index + 1]))
        for index in range(5)
    )
    strips = [pl.ds(first, half) for first in (0, half)]
    for rows in strips:
        grad.put(rows, total[rows, :])
    for rows in strips:
        matrix[rows, :] = dot_transposed(grad.high[rows, :], grad.high[...]) + (
            dot_transposed(grad.high[rows, :], grad.low[...])
            + dot_transposed(grad.low[rows, :], grad.high[...])
        )
    for place, (a, b) in enumerate(upper):
        term[place * TILE : (place + 1) * TILE, :] = matrix[
            a * TILE : (a + 1) * TILE, b * TILE : (b + 1) * TILE
        ]

    def to_server(index):
        return remote(
            term.at[rows_of(index)],
            terms_in.at[dp],
            back_send.at[index],
            back_recv.at[dp],
            band,
            2 * index + slot,
        )

    def from_server(index):
        return remote(
            term.at[rows_of(index)],
            terms_in.at[index],
            back_send.at[index],
            back_recv.at[index],
            index,
            served,
        )

    @pl.loop(0, blocks)
    def _(index):
        mine = jnp.logical_and(own_band, index == dp)

        @pl.when(jnp.logical_not(mine))
        def _():
            to_server(index).start()

        @pl.when(mine)
        def _():
            terms_in[index] = term[rows_of(index), :]

    @pl.loop(0, blocks)
    def _(index):
        @pl.when(jnp.logical_not(jnp.logical_and(own_band, index == dp)))
        def _():
            from_home(index).wait_recv()

    squares = jnp.zeros((1, 1), F32)
    for place, (a, b) in enumerate(upper):
        across = pl.ds(a * TILE, TILE), pl.ds(b * TILE, TILE)
        piece = pl.ds(place * TILE, TILE)
        value = DECAY * home_stat[piece, :] + GAIN / extent * term[piece, :]
        if a == b:
            value = value + jnp.where(diagonal(TILE, 0, TILE), F32(EPSILON), F32(0.0))
        else:
            matrix[across[1], across[0]] = value.T
        matrix[across[0], across[1]] = value
        squares = squares + (1.0 if a == b else 2.0) * jnp.sum(value * value, keepdims=True)

    scaling = 2.5 * lax.rsqrt(squares)
    start = jnp.sqrt(jnp.sqrt(scaling))

    def factor_of(value, rows):
        identity = diagonal(rows.size, rows.start, extent)
        return jnp.where(identity, 1.25 - 0.25 * value, -0.25 * value)

    for rows in strips:
        value = matrix[rows, :] * scaling
        current.put(rows, value)
        value = factor_of(value, rows)
        factor.put(rows, value)
        result.put(rows, start * value)

    def spread_terms():
        @pl.loop(0, blocks)
        def _(index):
            @pl.when(jnp.logical_not(jnp.logical_and(own_band, index == dp)))
            def _():
                from_server(index).wait_recv()

        owners = [owner_ref[served * blocks + index] for index in range(blocks)]

        @pl.loop(0, experts)
        def _(owner):
            at, there = jnp.int32(0), F32(0.0)
            for index in range(blocks):
                hit = owners[index] == owner
                at = jnp.where(hit, index, at)
                there = jnp.where(hit, F32(1.0), there)
            terms_out[owner] = there * terms_in[at]

        @pl.loop(1, experts)
        def _(step):
            to_owner(lax.rem(spot + step, experts)).start()

        owner_terms[slot, rows_of(band), :] = terms_out[spot]

    def to_owner(other):
        return remote(
            terms_out.at[other],
            owner_terms.at[slot, rows_of(band)],
            spread_send.at[other],
            spread_recv.at[spot],
            dp,
            other,
        )

    def from_owner(other):
        return remote(
            terms_out.at[other],
            owner_terms.at[lax.rem(other, 2), rows_of(other // 2)],
            spread_send.at[other],
            spread_recv.at[other],
            dp,
            other,
        )

    for repeat in range(ITERS - 1):
        for rows in strips:
            square.put(rows, product(factor, factor, rows))
        if repeat > 0:
            values = [product(result, factor, rows) for rows in strips]
            for rows, value in zip(strips, values):
                result.put(rows, value)
        for rows in strips:
            factor.put(rows, product(square, square, rows))
        values = [product(factor, current, rows) for rows in strips]
        for rows, value in zip(strips, values):
            current.put(rows, value)
            factor.put(rows, factor_of(value, rows))
        if repeat == 2:
            spread_terms()
    values = [product(result, factor, rows) for rows in strips]
    for rows, value in zip(strips, values):
        result.put(rows, value)
    for rows in strips:
        updates[rows, :] = product(result, grad, rows)

    width = extent // blocks

    def to_replica(index):
        return remote(
            updates.at[pl.ds(pl.multiple_of(index * width, width), width)],
            precond_out.at[dp],
            band_send.at[index],
            band_recv.at[dp],
            index,
            spot,
        )

    def from_replica(index):
        return remote(
            updates.at[pl.ds(0, width)],
            precond_out.at[index],
            band_send.at[index],
            band_recv.at[index],
            index,
            spot,
        )

    @pl.loop(1, blocks)
    def _(step):
        to_replica(lax.rem(dp + step, blocks)).start()

    keep = pltpu.make_async_copy(
        updates.at[pl.ds(pl.multiple_of(dp * width, width), width)], precond_out.at[dp], out_sem
    )
    keep.start()

    @pl.loop(1, experts)
    def _(step):
        from_owner(lax.rem(spot + step, experts)).wait_recv()

    for where in range(2):
        for place, (a, b) in enumerate(upper):
            value = GAIN / extent * owner_terms[where, place * TILE : (place + 1) * TILE, :]
            down, over = pl.ds(a * TILE, TILE), pl.ds(b * TILE, TILE)
            fresh_out[where, down, over] = DECAY * previous[where, down, over] + value
            if a != b:
                fresh_out[where, over, down] = DECAY * previous[where, over, down] + value.T

    for copy in crossing.values():
        copy.wait_send()
    for copy in (far_right, far_left, direct_right, direct_left, mixed_right, mixed_left):
        copy.wait_send()

    @pl.loop(1, experts)
    def _(step):
        other = lax.rem(spot + step, experts)
        to_plane(other).wait_send()
        to_owner(other).wait_send()

    @pl.loop(0, blocks)
    def _(index):
        @pl.when(jnp.logical_not(jnp.logical_and(own_band, index == dp)))
        def _():
            to_home(index).wait_send()
            to_server(index).wait_send()

    @pl.loop(1, blocks)
    def _(step):
        other = lax.rem(dp + step, blocks)
        to_replica(other).wait_send()
        from_replica(other).wait_recv()

    keep.wait()


def per_device(grad_parts, stat_owned, owner_list):
    experts = lax.axis_size("expert")
    blocks = lax.axis_size("dp")
    partials, previous = grad_parts[0], stat_owned[0]
    extent = partials.shape[1]
    tiles = extent // TILE
    packed_rows = tiles * (tiles + 1) // 2 * TILE
    depth = packed_rows // blocks
    half = extent // 2
    dma = pltpu.SemaphoreType.DMA
    square = (extent, extent)
    fresh, precond = pl.pallas_call(
        functools.partial(kernel, extent, blocks, experts),
        out_shape=[
            jax.ShapeDtypeStruct(previous.shape, F32),
            jax.ShapeDtypeStruct((blocks, extent // blocks, extent), F32),
        ],
        in_specs=[
            pl.BlockSpec(memory_space=pltpu.SMEM),
            pl.BlockSpec(memory_space=pl.ANY),
            pl.BlockSpec(memory_space=pl.ANY),
        ],
        out_specs=[pl.BlockSpec(memory_space=pltpu.VMEM), pl.BlockSpec(memory_space=pl.ANY)],
        scratch_shapes=[
            pltpu.VMEM((RING, *square), BF16),
            pltpu.VMEM((RING, *square), BF16),
            pltpu.VMEM(square, F32),
            pltpu.VMEM(square, F32),
            pltpu.VMEM(square, F32),
            pltpu.VMEM(square, F32),
            pltpu.VMEM((2, half, extent), F32),
            pltpu.VMEM((2, half, extent), F32),
            pltpu.VMEM((2, half, extent), F32),
            pltpu.VMEM((2, *square), F32),
            pltpu.VMEM((2, packed_rows, TILE), F32),
            pltpu.VMEM((experts, depth, TILE), F32),
            pltpu.VMEM((blocks, depth, TILE), F32),
            pltpu.VMEM((packed_rows, TILE), F32),
            pltpu.VMEM((packed_rows, TILE), F32),
            pltpu.VMEM((blocks, depth, TILE), F32),
            pltpu.VMEM((experts, depth, TILE), F32),
            pltpu.VMEM((2, packed_rows, TILE), F32),
            pltpu.VMEM(square, F32),
            pltpu.VMEM((10, *square), BF16),
            pltpu.VMEM(square, F32),
            dma((RING,)),
            dma(()),
            dma((RING,)),
            dma((RING,)),
            dma((6,)),
            dma((6,)),
            dma((experts,)),
            dma((experts,)),
            dma((blocks,)),
            dma((blocks,)),
            dma((blocks,)),
            dma((blocks,)),
            dma((experts,)),
            dma((experts,)),
            dma((blocks,)),
            dma((blocks,)),
            dma(()),
        ],
        compiler_params=pltpu.CompilerParams(
            collective_id=0, has_side_effects=True, vmem_limit_bytes=52 * 2**20
        ),
    )(owner_list, partials, previous)
    return (fresh[None], precond)


def solution(mesh):
    in_specs = (P("dp", "expert", None, None), P("expert", "dp", None, None), P())
    out_specs = (P("expert", "dp", None, None), P("expert", "dp", None))
    return jax.shard_map(
        per_device, mesh=mesh, in_specs=in_specs, out_specs=out_specs, check_vma=False
    )
```

```python
import functools

import jax
import jax.numpy as jnp
from jax import lax
from jax.experimental import pallas as pl
from jax.experimental.pallas import tpu as pltpu
from jax.sharding import PartitionSpec as P

ITERS = 6
EPSILON = 1e-06
DECAY = 0.9
GAIN = 0.1

MESH = pl.DeviceIdType.MESH
F32 = jnp.float32
BF16 = jnp.bfloat16
TILE = 128
RING = 4
CORES = 2
LEVELS = 16.0
LOWEST = -1600.0
PEAK = 32700.0
NOTE = 16


def remote(src, dst, send_sem, recv_sem, dp, expert):
    return pltpu.make_async_remote_copy(
        src_ref=src,
        dst_ref=dst,
        send_sem=send_sem,
        recv_sem=recv_sem,
        device_id={"dp": dp, "expert": expert},
        device_id_type=MESH,
    )


def split(value):
    high = value.astype(BF16)
    return high, (value - high.astype(F32)).astype(BF16)


def coded(value):
    peak = jnp.maximum(jnp.max(jnp.abs(value), axis=0, keepdims=True), 1e-30)
    level = jnp.maximum(jnp.ceil(LEVELS * jnp.log2(peak)), LOWEST)
    codes = jnp.round(value * (PEAK * jnp.exp2(level * (-1.0 / LEVELS))))
    return codes.astype(jnp.int32).astype(jnp.int16), level


def step_of(level):
    return jnp.exp2(level * (1.0 / LEVELS)) * (1.0 / PEAK)


def as_note(level, rows):
    return jnp.broadcast_to(level, (rows, level.shape[1])).astype(jnp.int32).astype(jnp.int16)


def floats(codes):
    return codes.astype(jnp.int32).astype(F32)


def decoded(piece, depth):
    level = floats(piece[depth : depth + NOTE, :])[:1, :]
    return floats(piece[:depth, :]) * step_of(level)


def dot(former, latter):
    return jnp.dot(former, latter, preferred_element_type=F32)


def dot_transposed(former, latter):
    return lax.dot_general(former, latter, (((1,), (1,)), ((), ())), preferred_element_type=F32)


def diagonal(rows, first, columns):
    across = lax.broadcasted_iota(jnp.int32, (rows, columns), 1)
    return lax.broadcasted_iota(jnp.int32, (rows, columns), 0) + first == across


class Pair:
    def __init__(self, refs):
        self.high, self.low = refs

    def put(self, rows, value):
        self.high[rows, :], self.low[rows, :] = split(value)


def product(former, latter, rows):
    return dot(former.high[rows, :], latter.high[...]) + (
        dot(former.high[rows, :], latter.low[...]) + dot(former.low[rows, :], latter.high[...])
    )


def kernel(
    extent,
    blocks,
    experts,
    owner_list,
    grads,
    stats,
    fresh_out,
    codes_out,
    owner_ref,
    own,
    part,
    far_sum,
    right_sum,
    left_sum,
    total,
    rx_far,
    rx_direct,
    rx_mixed,
    previous,
    fresh,
    packed,
    stat_codes,
    gathered,
    chosen,
    home_stat,
    term,
    term_codes,
    terms_in,
    terms_out,
    owner_terms,
    matrix,
    halves,
    band_codes,
    load_sem,
    stat_sem,
    owner_sem,
    core_send,
    core_recv,
    ring_send,
    ring_recv,
    plane_send,
    plane_recv,
    home_send,
    home_recv,
    back_send,
    back_recv,
    spread_send,
    spread_recv,
    band_send,
    band_recv,
    out_sem,
):
    dp = lax.axis_index("dp")
    spot = lax.axis_index("expert")
    x, core = dp // CORES, dp % CORES
    twin = x * CORES + 1 - core
    right = lax.rem(x + 1, RING) * CORES + core
    left = lax.rem(x + RING - 1, RING) * CORES + core
    slot, band = lax.rem(spot, 2), spot // 2
    served = 2 * dp + slot
    own_band = band == dp
    tiles = extent // TILE
    upper = [(a, b) for a in range(tiles) for b in range(a, tiles)]
    depth = len(upper) * TILE // blocks
    half = extent // 2

    def block_of(turn, which):
        return lax.rem(x + turn, RING) * CORES + which

    loads = {}
    for turn in (2, 1, 3, 0):
        loads[turn] = pltpu.make_async_copy(
            grads.at[block_of(turn, core)], own.at[turn], load_sem.at[turn]
        )
        loads[turn].start()
    stat_load = pltpu.make_async_copy(stats, previous, stat_sem)
    stat_load.start()
    owner_load = pltpu.make_async_copy(owner_list, owner_ref, owner_sem)
    owner_load.start()

    barrier = pltpu.get_barrier_semaphore()

    def greet(to_dp, to_expert):
        pl.semaphore_signal(
            barrier, inc=1, device_id={"dp": to_dp, "expert": to_expert}, device_id_type=MESH
        )

    @pl.loop(1, experts)
    def _(step):
        greet(dp, lax.rem(spot + step, experts))

    @pl.loop(1, blocks)
    def _(step):
        greet(lax.rem(dp + step, blocks), spot)

    @pl.loop(0, blocks)
    def _(step):
        @pl.when(jnp.logical_not(jnp.logical_and(own_band, step == dp)))
        def _():
            greet(step, served)
            greet(band, 2 * step + slot)

    def rows_of(index):
        return pl.ds(pl.multiple_of(index * depth, depth), depth)

    stat_load.wait()
    for where in range(2):
        for place, (a, b) in enumerate(upper):
            packed[where, place * TILE : (place + 1) * TILE, :] = previous[
                where, a * TILE : (a + 1) * TILE, b * TILE : (b + 1) * TILE
            ]

        @pl.loop(0, blocks)
        def _(index):
            codes, level = coded(packed[where, rows_of(index), :])
            stat_codes[where, index, :depth, :] = codes
            stat_codes[where, index, depth:, :] = as_note(level, NOTE)

    pl.semaphore_wait(barrier, experts - 1 + blocks - 1 + 2 * blocks - jnp.where(own_band, 2, 0))

    crossing = {}
    for turn in (2, 1, 3, 0):
        crossing[turn] = remote(
            grads.at[block_of(turn, 1 - core)],
            part.at[turn],
            core_send.at[turn],
            core_recv.at[turn],
            twin,
            spot,
        )
        crossing[turn].start()

    def pair_sum(turn, rows):
        return own[turn, rows, :].astype(F32) + part[turn, rows, :].astype(F32)

    top, bottom = pl.ds(0, half), pl.ds(half, half)

    def ring(index, src, dst, to):
        return remote(src, dst, ring_send.at[index], ring_recv.at[index], to, spot)

    loads[2].wait()
    crossing[2].wait_recv()
    far_sum[top, :] = pair_sum(2, top)
    far_right = ring(0, far_sum.at[top], rx_far.at[0], right)
    far_right.start()
    far_sum[bottom, :] = pair_sum(2, bottom)
    far_left = ring(1, far_sum.at[bottom], rx_far.at[1], left)
    far_left.start()

    loads[1].wait()
    crossing[1].wait_recv()
    right_sum[bottom, :] = pair_sum(1, bottom)
    direct_right = ring(2, right_sum.at[bottom], rx_direct.at[1], right)
    direct_right.start()
    loads[3].wait()
    crossing[3].wait_recv()
    left_sum[top, :] = pair_sum(3, top)
    direct_left = ring(3, left_sum.at[top], rx_direct.at[0], left)
    direct_left.start()

    def to_plane(other):
        return remote(
            stat_codes.at[lax.rem(other, 2), other // 2],
            gathered.at[spot],
            plane_send.at[other],
            plane_recv.at[spot],
            dp,
            other,
        )

    def from_plane(other):
        return remote(
            stat_codes.at[0, 0], gathered.at[other], plane_send.at[other], plane_recv.at[other], dp, other
        )

    @pl.loop(1, experts)
    def _(step):
        to_plane(lax.rem(spot + step, experts)).start()

    gathered[spot] = stat_codes[slot, band]

    right_sum[top, :] = pair_sum(1, top)
    left_sum[bottom, :] = pair_sum(3, bottom)
    loads[0].wait()
    crossing[0].wait_recv()
    total[...] = pair_sum(0, pl.ds(0, extent))

    far_right.wait_recv()
    right_sum[top, :] = right_sum[top, :] + rx_far[0]
    mixed_right = ring(4, right_sum.at[top], rx_mixed.at[0], right)
    mixed_right.start()
    far_left.wait_recv()
    left_sum[bottom, :] = left_sum[bottom, :] + rx_far[1]
    mixed_left = ring(5, left_sum.at[bottom], rx_mixed.at[1], left)
    mixed_left.start()

    @pl.loop(1, experts)
    def _(step):
        from_plane(lax.rem(spot + step, experts)).wait_recv()

    def to_home(index):
        return remote(
            chosen.at[index],
            home_stat.at[band],
            home_send.at[index],
            home_recv.at[band],
            index,
            served,
        )

    def from_home(index):
        return remote(
            chosen.at[index],
            home_stat.at[index],
            home_send.at[index],
            home_recv.at[index],
            band,
            2 * index + slot,
        )

    owner_load.wait()
    for index in range(blocks):
        chosen[index] = gathered[owner_ref[served * blocks + index]]

    @pl.loop(0, blocks)
    def _(index):
        mine = jnp.logical_and(own_band, index == dp)

        @pl.when(jnp.logical_not(mine))
        def _():
            to_home(index).start()

        @pl.when(mine)
        def _():
            home_stat[index] = chosen[index]

    direct_left.wait_recv()
    total[top, :] = total[top, :] + rx_direct[0]
    direct_right.wait_recv()
    total[bottom, :] = total[bottom, :] + rx_direct[1]
    mixed_right.wait_recv()
    total[top, :] = total[top, :] + rx_mixed[0]
    mixed_left.wait_recv()
    total[bottom, :] = total[bottom, :] + rx_mixed[1]

    grad, current, factor, result, square = (
        Pair((halves.at[2 * index], halves.at[2 * index + 1]))
        for index in range(5)
    )
    strips = [pl.ds(first, half) for first in (0, half)]
    for rows in strips:
        grad.put(rows, total[rows, :])
    for rows in strips:
        matrix[rows, :] = dot_transposed(grad.high[rows, :], grad.high[...]) + (
            dot_transposed(grad.high[rows, :], grad.low[...])
            + dot_transposed(grad.low[rows, :], grad.high[...])
        )
    for place, (a, b) in enumerate(upper):
        term[place * TILE : (place + 1) * TILE, :] = matrix[
            a * TILE : (a + 1) * TILE, b * TILE : (b + 1) * TILE
        ]

    @pl.loop(0, blocks)
    def _(index):
        codes, level = coded(term[rows_of(index), :])
        term_codes[index, :depth, :] = codes
        term_codes[index, depth:, :] = as_note(level, NOTE)

    def to_server(index):
        return remote(
            term_codes.at[index],
            terms_in.at[dp],
            back_send.at[index],
            back_recv.at[dp],
            band,
            2 * index + slot,
        )

    def from_server(index):
        return remote(
            term_codes.at[index],
            terms_in.at[index],
            back_send.at[index],
            back_recv.at[index],
            index,
            served,
        )

    @pl.loop(0, blocks)
    def _(index):
        mine = jnp.logical_and(own_band, index == dp)

        @pl.when(jnp.logical_not(mine))
        def _():
            to_server(index).start()

        @pl.when(mine)
        def _():
            terms_in[index] = term_codes[index]

    @pl.loop(0, blocks)
    def _(index):
        @pl.when(jnp.logical_not(jnp.logical_and(own_band, index == dp)))
        def _():
            from_home(index).wait_recv()

    for index in range(blocks):
        packed[0, index * depth : (index + 1) * depth, :] = decoded(home_stat.at[index], depth)

    squares = jnp.zeros((1, 1), F32)
    for place, (a, b) in enumerate(upper):
        across = pl.ds(a * TILE, TILE), pl.ds(b * TILE, TILE)
        piece = pl.ds(place * TILE, TILE)
        value = DECAY * packed[0, piece, :] + GAIN / extent * term[piece, :]
        if a == b:
            value = value + jnp.where(diagonal(TILE, 0, TILE), F32(EPSILON), F32(0.0))
        else:
            matrix[across[1], across[0]] = value.T
        matrix[across[0], across[1]] = value
        squares = squares + (1.0 if a == b else 2.0) * jnp.sum(value * value, keepdims=True)

    scaling = 2.5 * lax.rsqrt(squares)
    start = jnp.sqrt(jnp.sqrt(scaling))

    def factor_of(value, rows):
        identity = diagonal(rows.size, rows.start, extent)
        return jnp.where(identity, 1.25 - 0.25 * value, -0.25 * value)

    for rows in strips:
        value = matrix[rows, :] * scaling
        current.put(rows, value)
        value = factor_of(value, rows)
        factor.put(rows, value)
        result.put(rows, start * value)

    def spread_terms():
        @pl.loop(0, blocks)
        def _(index):
            @pl.when(jnp.logical_not(jnp.logical_and(own_band, index == dp)))
            def _():
                from_server(index).wait_recv()

        terms_in[blocks] = jnp.zeros(terms_in.shape[1:], jnp.int16)
        owners = [owner_ref[served * blocks + index] for index in range(blocks)]

        @pl.loop(0, experts)
        def _(owner):
            at = jnp.int32(blocks)
            for index in range(blocks):
                at = jnp.where(owners[index] == owner, index, at)
            terms_out[owner] = terms_in[at]

        @pl.loop(1, experts)
        def _(step):
            to_owner(lax.rem(spot + step, experts)).start()

        owner_terms[slot, band] = terms_out[spot]

    def to_owner(other):
        return remote(
            terms_out.at[other],
            owner_terms.at[slot, band],
            spread_send.at[other],
            spread_recv.at[spot],
            dp,
            other,
        )

    def from_owner(other):
        return remote(
            terms_out.at[other],
            owner_terms.at[lax.rem(other, 2), other // 2],
            spread_send.at[other],
            spread_recv.at[other],
            dp,
            other,
        )

    for repeat in range(ITERS - 1):
        for rows in strips:
            square.put(rows, product(factor, factor, rows))
        if repeat > 0:
            values = [product(result, factor, rows) for rows in strips]
            for rows, value in zip(strips, values):
                result.put(rows, value)
        for rows in strips:
            factor.put(rows, product(square, square, rows))
        values = [product(factor, current, rows) for rows in strips]
        for rows, value in zip(strips, values):
            current.put(rows, value)
            factor.put(rows, factor_of(value, rows))
        if repeat == 1:
            spread_terms()
    values = [product(result, factor, rows) for rows in strips]
    for rows, value in zip(strips, values):
        result.put(rows, value)

    width = extent // blocks
    inner = tiles * width

    def to_replica(index):
        return remote(
            band_codes.at[index],
            codes_out.at[dp],
            band_send.at[index],
            band_recv.at[dp],
            index,
            spot,
        )

    def from_replica(index):
        return remote(
            band_codes.at[index],
            codes_out.at[index],
            band_send.at[index],
            band_recv.at[index],
            index,
            spot,
        )

    keep = pltpu.make_async_copy(band_codes.at[dp], codes_out.at[dp], out_sem)
    line = lax.broadcasted_iota(jnp.int32, (NOTE, TILE), 0) // (NOTE // tiles)
    for rows in strips:
        value = product(result, grad, rows)
        for index in range(rows.start // width, (rows.start + rows.size) // width):
            first = index * width - rows.start
            note = jnp.zeros((NOTE, TILE), F32)
            for tile in range(tiles):
                codes, level = coded(value[first : first + width, tile * TILE : (tile + 1) * TILE])
                band_codes[index, tile * width : (tile + 1) * width, :] = codes
                note = jnp.where(line == tile, level, note)
            band_codes[index, inner:, :] = as_note(note, NOTE)

            @pl.when(index != dp)
            def _():
                to_replica(index).start()

            @pl.when(index == dp)
            def _():
                keep.start()

    @pl.loop(1, experts)
    def _(step):
        from_owner(lax.rem(spot + step, experts)).wait_recv()

    stores = []
    for where in range(2):
        for index in range(blocks):
            packed[where, index * depth : (index + 1) * depth, :] = decoded(
                owner_terms.at[where, index], depth
            )
        for place, (a, b) in enumerate(upper):
            value = GAIN / extent * packed[where, place * TILE : (place + 1) * TILE, :]
            down, over = pl.ds(a * TILE, TILE), pl.ds(b * TILE, TILE)
            fresh[where, down, over] = DECAY * previous[where, down, over] + value
            if a != b:
                fresh[where, over, down] = DECAY * previous[where, over, down] + value.T
        stores.append(pltpu.make_async_copy(fresh.at[where], fresh_out.at[where], load_sem.at[where]))
        stores[-1].start()

    for copy in crossing.values():
        copy.wait_send()
    for copy in (far_right, far_left, direct_right, direct_left, mixed_right, mixed_left):
        copy.wait_send()

    @pl.loop(1, experts)
    def _(step):
        other = lax.rem(spot + step, experts)
        to_plane(other).wait_send()
        to_owner(other).wait_send()

    @pl.loop(0, blocks)
    def _(index):
        @pl.when(jnp.logical_not(jnp.logical_and(own_band, index == dp)))
        def _():
            to_home(index).wait_send()
            to_server(index).wait_send()

    @pl.loop(1, blocks)
    def _(step):
        other = lax.rem(dp + step, blocks)
        to_replica(other).wait_send()
        from_replica(other).wait_recv()

    keep.wait()
    for copy in stores:
        copy.wait()


def finish(codes, fresh_in, fresh_out, precond, store_sem):
    store = pltpu.make_async_copy(fresh_in, fresh_out, store_sem)
    store.start()
    blocks, width, extent = precond.shape
    tiles = extent // TILE
    inner = tiles * width
    for index in range(blocks):
        levels = floats(codes[index, inner:, :])
        for tile in range(tiles):
            line = tile * (NOTE // tiles)
            precond[index, :, tile * TILE : (tile + 1) * TILE] = floats(
                codes[index, tile * width : (tile + 1) * width, :]
            ) * step_of(levels[line : line + 1, :])
    store.wait()


def per_device(grad_parts, stat_owned, owner_list):
    experts = lax.axis_size("expert")
    blocks = lax.axis_size("dp")
    partials, previous = grad_parts[0], stat_owned[0]
    extent = partials.shape[1]
    tiles = extent // TILE
    packed_rows = tiles * (tiles + 1) // 2 * TILE
    depth = packed_rows // blocks
    half = extent // 2
    dma = pltpu.SemaphoreType.DMA
    square = (extent, extent)
    width = extent // blocks
    inner = tiles * width + NOTE
    piece = (depth + NOTE, TILE)
    terms, codes = pl.pallas_call(
        functools.partial(kernel, extent, blocks, experts),
        out_shape=[
            jax.ShapeDtypeStruct(previous.shape, F32),
            jax.ShapeDtypeStruct((blocks, inner, TILE), jnp.int16),
        ],
        in_specs=[pl.BlockSpec(memory_space=pl.ANY)] * 3,
        out_specs=[pl.BlockSpec(memory_space=pl.ANY)] * 2,
        scratch_shapes=[
            pltpu.SMEM(owner_list.shape, jnp.int32),
            pltpu.VMEM((RING, *square), BF16),
            pltpu.VMEM((RING, *square), BF16),
            pltpu.VMEM(square, F32),
            pltpu.VMEM(square, F32),
            pltpu.VMEM(square, F32),
            pltpu.VMEM(square, F32),
            pltpu.VMEM((2, half, extent), F32),
            pltpu.VMEM((2, half, extent), F32),
            pltpu.VMEM((2, half, extent), F32),
            pltpu.VMEM((2, *square), F32),
            pltpu.VMEM((2, *square), F32),
            pltpu.VMEM((2, packed_rows, TILE), F32),
            pltpu.VMEM((2, blocks, *piece), jnp.int16),
            pltpu.VMEM((experts, *piece), jnp.int16),
            pltpu.VMEM((blocks, *piece), jnp.int16),
            pltpu.VMEM((blocks, *piece), jnp.int16),
            pltpu.VMEM((packed_rows, TILE), F32),
            pltpu.VMEM((blocks, *piece), jnp.int16),
            pltpu.VMEM((blocks + 1, *piece), jnp.int16),
            pltpu.VMEM((experts, *piece), jnp.int16),
            pltpu.VMEM((2, blocks, *piece), jnp.int16),
            pltpu.VMEM(square, F32),
            pltpu.VMEM((10, *square), BF16),
            pltpu.VMEM((blocks, inner, TILE), jnp.int16),
            dma((RING,)),
            dma(()),
            dma(()),
            dma((RING,)),
            dma((RING,)),
            dma((6,)),
            dma((6,)),
            dma((experts,)),
            dma((experts,)),
            dma((blocks,)),
            dma((blocks,)),
            dma((blocks,)),
            dma((blocks,)),
            dma((experts,)),
            dma((experts,)),
            dma((blocks,)),
            dma((blocks,)),
            dma(()),
        ],
        compiler_params=pltpu.CompilerParams(
            collective_id=0, has_side_effects=True, vmem_limit_bytes=60 * 2**20
        ),
    )(owner_list, partials, previous)
    fresh, precond = pl.pallas_call(
        finish,
        out_shape=[
            jax.ShapeDtypeStruct(previous.shape, F32),
            jax.ShapeDtypeStruct((blocks, width, extent), F32),
        ],
        in_specs=[pl.BlockSpec(memory_space=pltpu.VMEM)] * 2,
        out_specs=[pl.BlockSpec(memory_space=pl.ANY), pl.BlockSpec(memory_space=pltpu.VMEM)],
        scratch_shapes=[dma(())],
        compiler_params=pltpu.CompilerParams(vmem_limit_bytes=60 * 2**20),
    )(codes, terms)
    return (fresh[None], precond)


def solution(mesh):
    in_specs = (P("dp", "expert", None, None), P("expert", "dp", None, None), P())
    out_specs = (P("expert", "dp", None, None), P("expert", "dp", None))
    return jax.shard_map(
        per_device, mesh=mesh, in_specs=in_specs, out_specs=out_specs, check_vma=False
    )
```

```python
import functools

import jax
import jax.numpy as jnp
from jax import lax
from jax.experimental import pallas as pl
from jax.experimental.pallas import tpu as pltpu
from jax.sharding import PartitionSpec as P

ITERS = 6
EPSILON = 1e-06
DECAY = 0.9
GAIN = 0.1

MESH = pl.DeviceIdType.MESH
F32 = jnp.float32
BF16 = jnp.bfloat16
TILE = 128
RING = 4
CORES = 2
LEVELS = 16.0
LOWEST = -1600.0
PEAK = 32700.0
NOTE = 16


def remote(src, dst, send_sem, recv_sem, dp, expert):
    return pltpu.make_async_remote_copy(
        src_ref=src,
        dst_ref=dst,
        send_sem=send_sem,
        recv_sem=recv_sem,
        device_id={"dp": dp, "expert": expert},
        device_id_type=MESH,
    )


def split(value):
    high = value.astype(BF16)
    return high, (value - high.astype(F32)).astype(BF16)


def coded(value):
    peak = jnp.maximum(jnp.max(jnp.abs(value), axis=0, keepdims=True), 1e-30)
    level = jnp.maximum(jnp.ceil(LEVELS * jnp.log2(peak)), LOWEST)
    codes = jnp.round(value * (PEAK * jnp.exp2(level * (-1.0 / LEVELS))))
    return codes.astype(jnp.int32).astype(jnp.int16), level


def step_of(level):
    return jnp.exp2(level * (1.0 / LEVELS)) * (1.0 / PEAK)


def as_note(level, rows):
    return jnp.broadcast_to(level, (rows, level.shape[1])).astype(jnp.int32).astype(jnp.int16)


def floats(codes):
    return codes.astype(jnp.int32).astype(F32)


def decoded(piece, depth):
    level = floats(piece[depth : depth + NOTE, :])[:1, :]
    return floats(piece[:depth, :]) * step_of(level)


def dot(former, latter):
    return jnp.dot(former, latter, preferred_element_type=F32)


def dot_transposed(former, latter):
    return lax.dot_general(former, latter, (((1,), (1,)), ((), ())), preferred_element_type=F32)


def diagonal(rows, first, columns):
    across = lax.broadcasted_iota(jnp.int32, (rows, columns), 1)
    return lax.broadcasted_iota(jnp.int32, (rows, columns), 0) + first == across


class Pair:
    def __init__(self, high, low):
        self.high, self.low = high, low

    def put(self, rows, columns, value):
        self.high[rows, columns], self.low[rows, columns] = split(value)

    def put_symmetric(self, halves, corner, first, last):
        top, bottom = halves
        high, low = split(corner)
        self.high[top, bottom], self.low[top, bottom] = high, low
        self.high[bottom, top], self.low[bottom, top] = high.T, low.T
        self.put(top, top, first)
        self.put(bottom, bottom, last)


def product(former, latter, rows, columns, multiply=dot):
    def side(ref):
        return ref[:, columns] if multiply is dot else ref[columns, :]

    return multiply(former.high[rows, :], side(latter.high)) + (
        multiply(former.high[rows, :], side(latter.low))
        + multiply(former.low[rows, :], side(latter.high))
    )


def symmetric_product(former, latter, halves, multiply=dot):
    top, bottom = halves
    return [
        product(former, latter, rows, columns, multiply)
        for rows, columns in ((top, bottom), (top, top), (bottom, bottom))
    ]


def kernel(
    extent,
    blocks,
    experts,
    owner_list,
    grads,
    stats,
    fresh_out,
    codes_out,
    owner_ref,
    own,
    part,
    far_sum,
    right_sum,
    left_sum,
    total,
    rx_far,
    rx_direct,
    rx_mixed,
    previous,
    fresh,
    packed,
    stat_codes,
    gathered,
    chosen,
    home_stat,
    term,
    term_codes,
    terms_in,
    terms_out,
    owner_terms,
    matrix,
    halves,
    band_codes,
    load_sem,
    stat_sem,
    owner_sem,
    ready_sem,
    open_sem,
    core_send,
    core_recv,
    ring_send,
    ring_recv,
    plane_send,
    plane_recv,
    home_send,
    home_recv,
    back_send,
    back_recv,
    spread_send,
    spread_recv,
    band_send,
    band_recv,
    out_sem,
):
    dp = lax.axis_index("dp")
    spot = lax.axis_index("expert")
    x, core = dp // CORES, dp % CORES
    twin = x * CORES + 1 - core
    right = lax.rem(x + 1, RING) * CORES + core
    left = lax.rem(x + RING - 1, RING) * CORES + core
    slot, band = lax.rem(spot, 2), spot // 2
    served = 2 * dp + slot
    own_band = band == dp
    tiles = extent // TILE
    upper = [(a, b) for a in range(tiles) for b in range(a, tiles)]
    depth = len(upper) * TILE // blocks
    half = extent // 2

    def block_of(turn, which):
        return lax.rem(x + turn, RING) * CORES + which

    loads = {}
    for turn in (2, 1, 3, 0):
        loads[turn] = pltpu.make_async_copy(
            grads.at[block_of(turn, core)], own.at[turn], load_sem.at[turn]
        )
        loads[turn].start()
    stat_load = pltpu.make_async_copy(stats, previous, stat_sem)
    stat_load.start()
    owner_load = pltpu.make_async_copy(owner_list, owner_ref, owner_sem)
    owner_load.start()

    barrier = pltpu.get_barrier_semaphore()
    gate = dp == 0

    def tell(semaphore, to_dp, to_expert):
        pl.semaphore_signal(
            semaphore, inc=1, device_id={"dp": to_dp, "expert": to_expert}, device_id_type=MESH
        )

    @pl.loop(1, blocks)
    def _(step):
        other = lax.rem(dp + step, blocks)

        @pl.when(other != 0)
        def _():
            tell(barrier, other, spot)

    def rows_of(index):
        return pl.ds(pl.multiple_of(index * depth, depth), depth)

    stat_load.wait()
    for where in range(2):
        for place, (a, b) in enumerate(upper):
            packed[where, place * TILE : (place + 1) * TILE, :] = previous[
                where, a * TILE : (a + 1) * TILE, b * TILE : (b + 1) * TILE
            ]

        @pl.loop(0, blocks)
        def _(index):
            codes, level = coded(packed[where, rows_of(index), :])
            stat_codes[where, index, :depth, :] = codes
            stat_codes[where, index, depth:, :] = as_note(level, NOTE)

    @pl.when(jnp.logical_not(gate))
    def _():
        pl.semaphore_wait(barrier, blocks - 1)
        tell(ready_sem, 0, spot)

    @pl.when(gate)
    def _():
        pl.semaphore_wait(ready_sem, blocks - 1)

        @pl.loop(1, experts)
        def _(step):
            tell(barrier, 0, lax.rem(spot + step, experts))

    crossing = {}
    for turn in (2, 1, 3, 0):
        crossing[turn] = remote(
            grads.at[block_of(turn, 1 - core)],
            part.at[turn],
            core_send.at[turn],
            core_recv.at[turn],
            twin,
            spot,
        )
        crossing[turn].start()

    def pair_sum(turn, rows):
        return own[turn, rows, :].astype(F32) + part[turn, rows, :].astype(F32)

    top, bottom = pl.ds(0, half), pl.ds(half, half)

    def ring(index, src, dst, to):
        return remote(src, dst, ring_send.at[index], ring_recv.at[index], to, spot)

    loads[2].wait()
    crossing[2].wait_recv()
    far_sum[top, :] = pair_sum(2, top)
    far_right = ring(0, far_sum.at[top], rx_far.at[0], right)
    far_right.start()
    far_sum[bottom, :] = pair_sum(2, bottom)
    far_left = ring(1, far_sum.at[bottom], rx_far.at[1], left)
    far_left.start()

    loads[1].wait()
    crossing[1].wait_recv()
    right_sum[bottom, :] = pair_sum(1, bottom)
    direct_right = ring(2, right_sum.at[bottom], rx_direct.at[1], right)
    direct_right.start()
    loads[3].wait()
    crossing[3].wait_recv()
    left_sum[top, :] = pair_sum(3, top)
    direct_left = ring(3, left_sum.at[top], rx_direct.at[0], left)
    direct_left.start()

    def to_plane(other):
        return remote(
            stat_codes.at[lax.rem(other, 2), other // 2],
            gathered.at[spot],
            plane_send.at[other],
            plane_recv.at[spot],
            dp,
            other,
        )

    def from_plane(other):
        return remote(
            stat_codes.at[0, 0], gathered.at[other], plane_send.at[other], plane_recv.at[other], dp, other
        )

    @pl.when(gate)
    def _():
        pl.semaphore_wait(barrier, experts - 1)

        @pl.loop(1, blocks)
        def _(step):
            tell(open_sem, step, spot)

    @pl.when(jnp.logical_not(gate))
    def _():
        pl.semaphore_wait(open_sem, 1)

    @pl.loop(1, experts)
    def _(step):
        to_plane(lax.rem(spot + step, experts)).start()

    gathered[spot] = stat_codes[slot, band]

    right_sum[top, :] = pair_sum(1, top)
    left_sum[bottom, :] = pair_sum(3, bottom)
    loads[0].wait()
    crossing[0].wait_recv()
    total[...] = pair_sum(0, pl.ds(0, extent))

    far_right.wait_recv()
    right_sum[top, :] = right_sum[top, :] + rx_far[0]
    mixed_right = ring(4, right_sum.at[top], rx_mixed.at[0], right)
    mixed_right.start()
    far_left.wait_recv()
    left_sum[bottom, :] = left_sum[bottom, :] + rx_far[1]
    mixed_left = ring(5, left_sum.at[bottom], rx_mixed.at[1], left)
    mixed_left.start()

    @pl.loop(1, experts)
    def _(step):
        from_plane(lax.rem(spot + step, experts)).wait_recv()

    def to_home(index):
        return remote(
            chosen.at[index],
            home_stat.at[band],
            home_send.at[index],
            home_recv.at[band],
            index,
            served,
        )

    def from_home(index):
        return remote(
            chosen.at[index],
            home_stat.at[index],
            home_send.at[index],
            home_recv.at[index],
            band,
            2 * index + slot,
        )

    owner_load.wait()
    for index in range(blocks):
        chosen[index] = gathered[owner_ref[served * blocks + index]]

    @pl.loop(0, blocks)
    def _(index):
        mine = jnp.logical_and(own_band, index == dp)

        @pl.when(jnp.logical_not(mine))
        def _():
            to_home(index).start()

        @pl.when(mine)
        def _():
            home_stat[index] = chosen[index]

    direct_left.wait_recv()
    total[top, :] = total[top, :] + rx_direct[0]
    direct_right.wait_recv()
    total[bottom, :] = total[bottom, :] + rx_direct[1]
    mixed_right.wait_recv()
    total[top, :] = total[top, :] + rx_mixed[0]
    mixed_left.wait_recv()
    total[bottom, :] = total[bottom, :] + rx_mixed[1]

    grad, current, factor, result, square = (
        Pair(halves.at[2 * index], halves.at[2 * index + 1]) for index in range(5)
    )
    strips = [top, bottom]
    whole = pl.ds(0, extent)
    for rows in strips:
        grad.put(rows, whole, total[rows, :])
    corner, first, last = symmetric_product(grad, grad, strips, dot_transposed)
    matrix[top, bottom] = corner
    matrix[top, top] = first
    matrix[bottom, bottom] = last
    for place, (a, b) in enumerate(upper):
        term[place * TILE : (place + 1) * TILE, :] = matrix[
            a * TILE : (a + 1) * TILE, b * TILE : (b + 1) * TILE
        ]

    @pl.loop(0, blocks)
    def _(index):
        codes, level = coded(term[rows_of(index), :])
        term_codes[index, :depth, :] = codes
        term_codes[index, depth:, :] = as_note(level, NOTE)

    def to_server(index):
        return remote(
            term_codes.at[index],
            terms_in.at[dp],
            back_send.at[index],
            back_recv.at[dp],
            band,
            2 * index + slot,
        )

    def from_server(index):
        return remote(
            term_codes.at[index],
            terms_in.at[index],
            back_send.at[index],
            back_recv.at[index],
            index,
            served,
        )

    @pl.loop(0, blocks)
    def _(index):
        mine = jnp.logical_and(own_band, index == dp)

        @pl.when(jnp.logical_not(mine))
        def _():
            to_server(index).start()

        @pl.when(mine)
        def _():
            terms_in[index] = term_codes[index]

    @pl.loop(0, blocks)
    def _(index):
        @pl.when(jnp.logical_not(jnp.logical_and(own_band, index == dp)))
        def _():
            from_home(index).wait_recv()

    for index in range(blocks):
        packed[0, index * depth : (index + 1) * depth, :] = decoded(home_stat.at[index], depth)

    squares = jnp.zeros((1, 1), F32)
    for place, (a, b) in enumerate(upper):
        across = pl.ds(a * TILE, TILE), pl.ds(b * TILE, TILE)
        piece = pl.ds(place * TILE, TILE)
        value = DECAY * packed[0, piece, :] + GAIN / extent * term[piece, :]
        if a == b:
            value = value + jnp.where(diagonal(TILE, 0, TILE), F32(EPSILON), F32(0.0))
        elif a // (tiles // 2) == b // (tiles // 2):
            matrix[across[1], across[0]] = value.T
        matrix[across[0], across[1]] = value
        squares = squares + (1.0 if a == b else 2.0) * jnp.sum(value * value, keepdims=True)

    scaling = 2.5 * lax.rsqrt(squares)
    start = jnp.sqrt(jnp.sqrt(scaling))

    def factors_of(corner, first, last):
        identity = diagonal(half, 0, half)
        return [-0.25 * corner] + [
            jnp.where(identity, 1.25 - 0.25 * block, -0.25 * block) for block in (first, last)
        ]

    scaled = [
        matrix[rows, columns] * scaling
        for rows, columns in ((top, bottom), (top, top), (bottom, bottom))
    ]
    current.put_symmetric(strips, *scaled)
    scaled = factors_of(*scaled)
    factor.put_symmetric(strips, *scaled)
    result.put_symmetric(strips, *[start * block for block in scaled])

    def spread_terms():
        @pl.loop(0, blocks)
        def _(index):
            @pl.when(jnp.logical_not(jnp.logical_and(own_band, index == dp)))
            def _():
                from_server(index).wait_recv()

        terms_in[blocks] = jnp.zeros(terms_in.shape[1:], jnp.int16)
        owners = [owner_ref[served * blocks + index] for index in range(blocks)]

        @pl.loop(0, experts)
        def _(owner):
            at = jnp.int32(blocks)
            for index in range(blocks):
                at = jnp.where(owners[index] == owner, index, at)
            terms_out[owner] = terms_in[at]

        @pl.loop(1, experts)
        def _(step):
            to_owner(lax.rem(spot + step, experts)).start()

        owner_terms[slot, band] = terms_out[spot]

    def to_owner(other):
        return remote(
            terms_out.at[other],
            owner_terms.at[slot, band],
            spread_send.at[other],
            spread_recv.at[spot],
            dp,
            other,
        )

    def from_owner(other):
        return remote(
            terms_out.at[other],
            owner_terms.at[lax.rem(other, 2), other // 2],
            spread_send.at[other],
            spread_recv.at[other],
            dp,
            other,
        )

    for repeat in range(ITERS - 1):
        squared = symmetric_product(factor, factor, strips)
        if repeat > 0:
            advanced = symmetric_product(result, factor, strips)
        square.put_symmetric(strips, *squared)
        fourth = symmetric_product(square, square, strips)
        if repeat > 0:
            result.put_symmetric(strips, *advanced)
        factor.put_symmetric(strips, *fourth)
        following = symmetric_product(factor, current, strips)
        current.put_symmetric(strips, *following)
        factor.put_symmetric(strips, *factors_of(*following))
        if repeat == 2:
            spread_terms()
    result.put_symmetric(strips, *symmetric_product(result, factor, strips))

    width = extent // blocks
    inner = tiles * width

    def to_replica(index):
        return remote(
            band_codes.at[index],
            codes_out.at[dp],
            band_send.at[index],
            band_recv.at[dp],
            index,
            spot,
        )

    def from_replica(index):
        return remote(
            band_codes.at[index],
            codes_out.at[index],
            band_send.at[index],
            band_recv.at[index],
            index,
            spot,
        )

    keep = pltpu.make_async_copy(band_codes.at[dp], codes_out.at[dp], out_sem)
    line = lax.broadcasted_iota(jnp.int32, (NOTE, TILE), 0) // (NOTE // tiles)
    for rows in strips:
        value = product(result, grad, rows, whole)
        for index in range(rows.start // width, (rows.start + rows.size) // width):
            first = index * width - rows.start
            note = jnp.zeros((NOTE, TILE), F32)
            for tile in range(tiles):
                codes, level = coded(value[first : first + width, tile * TILE : (tile + 1) * TILE])
                band_codes[index, tile * width : (tile + 1) * width, :] = codes
                note = jnp.where(line == tile, level, note)
            band_codes[index, inner:, :] = as_note(note, NOTE)

            @pl.when(index != dp)
            def _():
                to_replica(index).start()

            @pl.when(index == dp)
            def _():
                keep.start()

    @pl.loop(1, experts)
    def _(step):
        from_owner(lax.rem(spot + step, experts)).wait_recv()

    stores = []
    for where in range(2):
        for index in range(blocks):
            packed[where, index * depth : (index + 1) * depth, :] = decoded(
                owner_terms.at[where, index], depth
            )
        for place, (a, b) in enumerate(upper):
            value = GAIN / extent * packed[where, place * TILE : (place + 1) * TILE, :]
            down, over = pl.ds(a * TILE, TILE), pl.ds(b * TILE, TILE)
            fresh[where, down, over] = DECAY * previous[where, down, over] + value
            if a != b:
                fresh[where, over, down] = DECAY * previous[where, over, down] + value.T
        stores.append(pltpu.make_async_copy(fresh.at[where], fresh_out.at[where], load_sem.at[where]))
        stores[-1].start()

    for copy in crossing.values():
        copy.wait_send()
    for copy in (far_right, far_left, direct_right, direct_left, mixed_right, mixed_left):
        copy.wait_send()

    @pl.loop(1, experts)
    def _(step):
        other = lax.rem(spot + step, experts)
        to_plane(other).wait_send()
        to_owner(other).wait_send()

    @pl.loop(0, blocks)
    def _(index):
        @pl.when(jnp.logical_not(jnp.logical_and(own_band, index == dp)))
        def _():
            to_home(index).wait_send()
            to_server(index).wait_send()

    @pl.loop(1, blocks)
    def _(step):
        other = lax.rem(dp + step, blocks)
        to_replica(other).wait_send()
        from_replica(other).wait_recv()

    keep.wait()
    for copy in stores:
        copy.wait()


def finish(codes, fresh_in, fresh_out, precond_out, taken, passing, precond, load_sem, store_sem):
    load_codes = pltpu.make_async_copy(codes, taken, load_sem.at[2])
    load_codes.start()
    loads = [
        pltpu.make_async_copy(fresh_in.at[where], passing.at[where], load_sem.at[where])
        for where in range(2)
    ]
    for load in loads:
        load.start()
    blocks, width, extent = precond.shape
    tiles = extent // TILE
    inner = tiles * width
    stores = []
    load_codes.wait()
    for part in range(2):
        for index in range(part * blocks // 2, (part + 1) * blocks // 2):
            levels = floats(taken[index, inner:, :])
            for tile in range(tiles):
                line = tile * (NOTE // tiles)
                precond[index, :, tile * TILE : (tile + 1) * TILE] = floats(
                    taken[index, tile * width : (tile + 1) * width, :]
                ) * step_of(levels[line : line + 1, :])
        here = pl.ds(part * blocks // 2, blocks // 2)
        stores.append(
            pltpu.make_async_copy(precond.at[here], precond_out.at[here], store_sem.at[2 + part])
        )
        stores[-1].start()
        loads[part].wait()
        stores.append(
            pltpu.make_async_copy(passing.at[part], fresh_out.at[part], store_sem.at[part])
        )
        stores[-1].start()
    for store in stores:
        store.wait()


def per_device(grad_parts, stat_owned, owner_list):
    experts = lax.axis_size("expert")
    blocks = lax.axis_size("dp")
    partials, previous = grad_parts[0], stat_owned[0]
    extent = partials.shape[1]
    tiles = extent // TILE
    packed_rows = tiles * (tiles + 1) // 2 * TILE
    depth = packed_rows // blocks
    half = extent // 2
    dma = pltpu.SemaphoreType.DMA
    square = (extent, extent)
    width = extent // blocks
    inner = tiles * width + NOTE
    piece = (depth + NOTE, TILE)
    terms, codes = pl.pallas_call(
        functools.partial(kernel, extent, blocks, experts),
        out_shape=[
            jax.ShapeDtypeStruct(previous.shape, F32),
            jax.ShapeDtypeStruct((blocks, inner, TILE), jnp.int16),
        ],
        in_specs=[pl.BlockSpec(memory_space=pl.ANY)] * 3,
        out_specs=[pl.BlockSpec(memory_space=pl.ANY)] * 2,
        scratch_shapes=[
            pltpu.SMEM(owner_list.shape, jnp.int32),
            pltpu.VMEM((RING, *square), BF16),
            pltpu.VMEM((RING, *square), BF16),
            pltpu.VMEM(square, F32),
            pltpu.VMEM(square, F32),
            pltpu.VMEM(square, F32),
            pltpu.VMEM(square, F32),
            pltpu.VMEM((2, half, extent), F32),
            pltpu.VMEM((2, half, extent), F32),
            pltpu.VMEM((2, half, extent), F32),
            pltpu.VMEM((2, *square), F32),
            pltpu.VMEM((2, *square), F32),
            pltpu.VMEM((2, packed_rows, TILE), F32),
            pltpu.VMEM((2, blocks, *piece), jnp.int16),
            pltpu.VMEM((experts, *piece), jnp.int16),
            pltpu.VMEM((blocks, *piece), jnp.int16),
            pltpu.VMEM((blocks, *piece), jnp.int16),
            pltpu.VMEM((packed_rows, TILE), F32),
            pltpu.VMEM((blocks, *piece), jnp.int16),
            pltpu.VMEM((blocks + 1, *piece), jnp.int16),
            pltpu.VMEM((experts, *piece), jnp.int16),
            pltpu.VMEM((2, blocks, *piece), jnp.int16),
            pltpu.VMEM(square, F32),
            pltpu.VMEM((10, *square), BF16),
            pltpu.VMEM((blocks, inner, TILE), jnp.int16),
            dma((RING,)),
            dma(()),
            dma(()),
            pltpu.SemaphoreType.REGULAR,
            pltpu.SemaphoreType.REGULAR,
            dma((RING,)),
            dma((RING,)),
            dma((6,)),
            dma((6,)),
            dma((experts,)),
            dma((experts,)),
            dma((blocks,)),
            dma((blocks,)),
            dma((blocks,)),
            dma((blocks,)),
            dma((experts,)),
            dma((experts,)),
            dma((blocks,)),
            dma((blocks,)),
            dma(()),
        ],
        compiler_params=pltpu.CompilerParams(
            collective_id=0, has_side_effects=True, vmem_limit_bytes=60 * 2**20
        ),
    )(owner_list, partials, previous)
    fresh, precond = pl.pallas_call(
        finish,
        out_shape=[
            jax.ShapeDtypeStruct(previous.shape, F32),
            jax.ShapeDtypeStruct((blocks, width, extent), F32),
        ],
        in_specs=[pl.BlockSpec(memory_space=pl.ANY)] * 2,
        out_specs=[pl.BlockSpec(memory_space=pl.ANY)] * 2,
        scratch_shapes=[
            pltpu.VMEM(codes.shape, jnp.int16),
            pltpu.VMEM(previous.shape, F32),
            pltpu.VMEM((blocks, width, extent), F32),
            dma((3,)),
            dma((4,)),
        ],
        compiler_params=pltpu.CompilerParams(vmem_limit_bytes=60 * 2**20),
    )(codes, terms)
    return (fresh[None], precond)


def solution(mesh):
    in_specs = (P("dp", "expert", None, None), P("expert", "dp", None, None), P())
    out_specs = (P("expert", "dp", None, None), P("expert", "dp", None))
    return jax.shard_map(
        per_device, mesh=mesh, in_specs=in_specs, out_specs=out_specs, check_vma=False
    )
```

```python
import functools

import jax
import jax.numpy as jnp
from jax import lax
from jax.experimental import pallas as pl
from jax.experimental.pallas import tpu as pltpu
from jax.sharding import PartitionSpec as P

ITERS = 6
EPSILON = 1e-06
DECAY = 0.9
GAIN = 0.1

MESH = pl.DeviceIdType.MESH
F32 = jnp.float32
BF16 = jnp.bfloat16
TILE = 128
RING = 4
CORES = 2
LEVELS = 16.0
LOWEST = -1600.0
PEAK = 32700.0
NOTE = 16
WIDE = 22.0
BYTE = 256
HALFWAY = 32768


def remote(src, dst, send_sem, recv_sem, dp, expert):
    return pltpu.make_async_remote_copy(
        src_ref=src,
        dst_ref=dst,
        send_sem=send_sem,
        recv_sem=recv_sem,
        device_id={"dp": dp, "expert": expert},
        device_id_type=MESH,
    )


def split(value):
    high = value.astype(BF16)
    return high, (value - high.astype(F32)).astype(BF16)


def coded(value):
    peak = jnp.maximum(jnp.max(jnp.abs(value), axis=0, keepdims=True), 1e-30)
    level = jnp.maximum(jnp.ceil(LEVELS * jnp.log2(peak)), LOWEST)
    codes = jnp.round(value * (PEAK * jnp.exp2(level * (-1.0 / LEVELS))))
    return codes.astype(jnp.int32).astype(jnp.int16), level


def step_of(level):
    return jnp.exp2(level * (1.0 / LEVELS)) * (1.0 / PEAK)


def as_note(level, rows):
    return jnp.broadcast_to(level, (rows, level.shape[1])).astype(jnp.int32).astype(jnp.int16)


def floats(codes):
    return codes.astype(jnp.int32).astype(F32)


def decoded(piece, depth):
    level = floats(piece[depth : depth + NOTE, :])[:1, :]
    return floats(piece[:depth, :]) * step_of(level)


def wide_coded(piece, tile, value):
    rows = value.shape[0]
    peak = jnp.maximum(jnp.max(jnp.abs(value), axis=0, keepdims=True), 1e-30)
    level = jnp.ceil(jnp.log2(peak))
    codes = jnp.round(value * jnp.exp2(WIDE - level)).astype(jnp.int32)
    first = tile * (rows + rows // 2)
    piece[first : first + rows, :] = (codes >> 8).astype(jnp.int16)
    low = codes & (BYTE - 1)
    low = low[: rows // 2, :] + (low[rows // 2 :, :] << 8) - HALFWAY
    piece[first + rows : first + rows + rows // 2, :] = low.astype(jnp.int16)
    return level


def wide_decoded(piece, tile, rows, tiles):
    first = tile * (rows + rows // 2)
    note = tiles * (rows + rows // 2)
    line = tile * (NOTE // tiles)
    level = floats(piece[note : note + NOTE, :])[line : line + 1, :]
    low = piece[first + rows : first + rows + rows // 2, :].astype(jnp.int32) + HALFWAY
    low = jnp.concatenate([low & (BYTE - 1), low >> 8], axis=0)
    codes = (piece[first : first + rows, :].astype(jnp.int32) << 8) + low
    return codes.astype(F32) * jnp.exp2(level - WIDE)


def dot(former, latter):
    return jnp.dot(former, latter, preferred_element_type=F32)


def dot_transposed(former, latter):
    return lax.dot_general(former, latter, (((1,), (1,)), ((), ())), preferred_element_type=F32)


def diagonal(rows, first, columns):
    across = lax.broadcasted_iota(jnp.int32, (rows, columns), 1)
    return lax.broadcasted_iota(jnp.int32, (rows, columns), 0) + first == across


class Pair:
    def __init__(self, high, low):
        self.high, self.low = high, low

    def put(self, rows, columns, value):
        self.high[rows, columns], self.low[rows, columns] = split(value)

    def put_symmetric(self, halves, corner, first, last):
        top, bottom = halves
        high, low = split(corner)
        self.high[top, bottom], self.low[top, bottom] = high, low
        self.high[bottom, top], self.low[bottom, top] = high.T, low.T
        self.put(top, top, first)
        self.put(bottom, bottom, last)


def product(former, latter, rows, columns, multiply=dot):
    def side(ref):
        return ref[:, columns] if multiply is dot else ref[columns, :]

    return multiply(former.high[rows, :], side(latter.high)) + (
        multiply(former.high[rows, :], side(latter.low))
        + multiply(former.low[rows, :], side(latter.high))
    )


def symmetric_product(former, latter, halves, multiply=dot):
    top, bottom = halves
    return [
        product(former, latter, rows, columns, multiply)
        for rows, columns in ((top, bottom), (top, top), (bottom, bottom))
    ]


def kernel(
    extent,
    blocks,
    experts,
    owner_list,
    grads,
    stats,
    fresh_out,
    codes_out,
    owner_ref,
    own,
    part,
    total,
    sent,
    received,
    previous,
    fresh,
    packed,
    stat_codes,
    gathered,
    chosen,
    home_stat,
    term,
    term_codes,
    terms_in,
    terms_out,
    owner_terms,
    matrix,
    halves,
    band_codes,
    load_sem,
    stat_sem,
    owner_sem,
    ready_sem,
    open_sem,
    core_send,
    core_recv,
    ring_send,
    ring_recv,
    plane_send,
    plane_recv,
    home_send,
    home_recv,
    back_send,
    back_recv,
    spread_send,
    spread_recv,
    band_send,
    band_recv,
    out_sem,
):
    dp = lax.axis_index("dp")
    spot = lax.axis_index("expert")
    x, core = dp // CORES, dp % CORES
    twin = x * CORES + 1 - core
    right = lax.rem(x + 1, RING) * CORES + core
    left = lax.rem(x + RING - 1, RING) * CORES + core
    slot, band = lax.rem(spot, 2), spot // 2
    served = 2 * dp + slot
    own_band = band == dp
    tiles = extent // TILE
    upper = [(a, b) for a in range(tiles) for b in range(a, tiles)]
    depth = len(upper) * TILE // blocks
    half = extent // 2

    def block_of(turn, which):
        return lax.rem(x + turn, RING) * CORES + which

    loads = {}
    for turn in (2, 1, 3, 0):
        loads[turn] = pltpu.make_async_copy(
            grads.at[block_of(turn, core)], own.at[turn], load_sem.at[turn]
        )
        loads[turn].start()
    stat_load = pltpu.make_async_copy(stats, previous, stat_sem)
    stat_load.start()
    owner_load = pltpu.make_async_copy(owner_list, owner_ref, owner_sem)
    owner_load.start()

    barrier = pltpu.get_barrier_semaphore()
    gate = dp == 0

    def tell(semaphore, to_dp, to_expert):
        pl.semaphore_signal(
            semaphore, inc=1, device_id={"dp": to_dp, "expert": to_expert}, device_id_type=MESH
        )

    @pl.loop(1, blocks)
    def _(step):
        other = lax.rem(dp + step, blocks)

        @pl.when(other != 0)
        def _():
            tell(barrier, other, spot)

    def rows_of(index):
        return pl.ds(pl.multiple_of(index * depth, depth), depth)

    stat_load.wait()
    for where in range(2):
        for place, (a, b) in enumerate(upper):
            packed[where, place * TILE : (place + 1) * TILE, :] = previous[
                where, a * TILE : (a + 1) * TILE, b * TILE : (b + 1) * TILE
            ]

        @pl.loop(0, blocks)
        def _(index):
            codes, level = coded(packed[where, rows_of(index), :])
            stat_codes[where, index, :depth, :] = codes
            stat_codes[where, index, depth:, :] = as_note(level, NOTE)

    @pl.when(jnp.logical_not(gate))
    def _():
        pl.semaphore_wait(barrier, blocks - 1)
        tell(ready_sem, 0, spot)

    @pl.when(gate)
    def _():
        pl.semaphore_wait(ready_sem, blocks - 1)

        @pl.loop(1, experts)
        def _(step):
            tell(barrier, 0, lax.rem(spot + step, experts))

    crossing = {}
    for turn in (2, 1, 3, 0):
        crossing[turn] = remote(
            grads.at[block_of(turn, 1 - core)],
            part.at[turn],
            core_send.at[turn],
            core_recv.at[turn],
            twin,
            spot,
        )
        crossing[turn].start()

    def pair_sum(turn, rows, columns):
        return own[turn, rows, columns].astype(F32) + part[turn, rows, columns].astype(F32)

    top, bottom = pl.ds(0, half), pl.ds(half, half)
    line = lax.broadcasted_iota(jnp.int32, (NOTE, TILE), 0) // (NOTE // tiles)

    def ring(index, to):
        return remote(
            sent.at[index], received.at[index], ring_send.at[index], ring_recv.at[index], to, spot
        )

    def pass_on(index, to, turn, rows, arrived=None):
        note = jnp.zeros((NOTE, TILE), F32)
        for tile in range(tiles):
            value = pair_sum(turn, rows, pl.ds(tile * TILE, TILE))
            if arrived is not None:
                value = value + wide_decoded(received.at[arrived], tile, half, tiles)
            note = jnp.where(line == tile, wide_coded(sent.at[index], tile, value), note)
        sent[index, tiles * (half + half // 2) :, :] = as_note(note, NOTE)
        copy = ring(index, to)
        copy.start()
        return copy

    loads[2].wait()
    crossing[2].wait_recv()
    far_right = pass_on(0, right, 2, top)
    far_left = pass_on(1, left, 2, bottom)
    loads[1].wait()
    crossing[1].wait_recv()
    direct_right = pass_on(2, right, 1, bottom)
    loads[3].wait()
    crossing[3].wait_recv()
    direct_left = pass_on(3, left, 3, top)

    def to_plane(other):
        return remote(
            stat_codes.at[lax.rem(other, 2), other // 2],
            gathered.at[spot],
            plane_send.at[other],
            plane_recv.at[spot],
            dp,
            other,
        )

    def from_plane(other):
        return remote(
            stat_codes.at[0, 0], gathered.at[other], plane_send.at[other], plane_recv.at[other], dp, other
        )

    @pl.when(gate)
    def _():
        pl.semaphore_wait(barrier, experts - 1)

        @pl.loop(1, blocks)
        def _(step):
            tell(open_sem, step, spot)

    @pl.when(jnp.logical_not(gate))
    def _():
        pl.semaphore_wait(open_sem, 1)

    @pl.loop(1, experts)
    def _(step):
        to_plane(lax.rem(spot + step, experts)).start()

    gathered[spot] = stat_codes[slot, band]

    loads[0].wait()
    crossing[0].wait_recv()
    for rows in (top, bottom):
        total[rows, :] = pair_sum(0, rows, pl.ds(0, extent))

    far_right.wait_recv()
    mixed_right = pass_on(4, right, 1, top, 0)
    far_left.wait_recv()
    mixed_left = pass_on(5, left, 3, bottom, 1)

    @pl.loop(1, experts)
    def _(step):
        from_plane(lax.rem(spot + step, experts)).wait_recv()

    def to_home(index):
        return remote(
            chosen.at[index],
            home_stat.at[band],
            home_send.at[index],
            home_recv.at[band],
            index,
            served,
        )

    def from_home(index):
        return remote(
            chosen.at[index],
            home_stat.at[index],
            home_send.at[index],
            home_recv.at[index],
            band,
            2 * index + slot,
        )

    owner_load.wait()
    for index in range(blocks):
        chosen[index] = gathered[owner_ref[served * blocks + index]]

    @pl.loop(0, blocks)
    def _(index):
        mine = jnp.logical_and(own_band, index == dp)

        @pl.when(jnp.logical_not(mine))
        def _():
            to_home(index).start()

        @pl.when(mine)
        def _():
            home_stat[index] = chosen[index]

    for copy, index, rows in (
        (direct_left, 3, top),
        (direct_right, 2, bottom),
        (mixed_right, 4, top),
        (mixed_left, 5, bottom),
    ):
        copy.wait_recv()
        for tile in range(tiles):
            columns = pl.ds(tile * TILE, TILE)
            total[rows, columns] = total[rows, columns] + wide_decoded(
                received.at[index], tile, half, tiles
            )

    grad, current, factor, result, square = (
        Pair(halves.at[2 * index], halves.at[2 * index + 1]) for index in range(5)
    )
    strips = [top, bottom]
    whole = pl.ds(0, extent)
    for rows in strips:
        grad.put(rows, whole, total[rows, :])
    corner, first, last = symmetric_product(grad, grad, strips, dot_transposed)
    matrix[top, bottom] = corner
    matrix[top, top] = first
    matrix[bottom, bottom] = last
    for place, (a, b) in enumerate(upper):
        term[place * TILE : (place + 1) * TILE, :] = matrix[
            a * TILE : (a + 1) * TILE, b * TILE : (b + 1) * TILE
        ]

    @pl.loop(0, blocks)
    def _(index):
        codes, level = coded(term[rows_of(index), :])
        term_codes[index, :depth, :] = codes
        term_codes[index, depth:, :] = as_note(level, NOTE)

    def to_server(index):
        return remote(
            term_codes.at[index],
            terms_in.at[dp],
            back_send.at[index],
            back_recv.at[dp],
            band,
            2 * index + slot,
        )

    def from_server(index):
        return remote(
            term_codes.at[index],
            terms_in.at[index],
            back_send.at[index],
            back_recv.at[index],
            index,
            served,
        )

    @pl.loop(0, blocks)
    def _(index):
        mine = jnp.logical_and(own_band, index == dp)

        @pl.when(jnp.logical_not(mine))
        def _():
            to_server(index).start()

        @pl.when(mine)
        def _():
            terms_in[index] = term_codes[index]

    @pl.loop(0, blocks)
    def _(index):
        @pl.when(jnp.logical_not(jnp.logical_and(own_band, index == dp)))
        def _():
            from_home(index).wait_recv()

    for index in range(blocks):
        packed[0, index * depth : (index + 1) * depth, :] = decoded(home_stat.at[index], depth)

    squares = jnp.zeros((1, 1), F32)
    for place, (a, b) in enumerate(upper):
        across = pl.ds(a * TILE, TILE), pl.ds(b * TILE, TILE)
        piece = pl.ds(place * TILE, TILE)
        value = DECAY * packed[0, piece, :] + GAIN / extent * term[piece, :]
        if a == b:
            value = value + jnp.where(diagonal(TILE, 0, TILE), F32(EPSILON), F32(0.0))
        elif a // (tiles // 2) == b // (tiles // 2):
            matrix[across[1], across[0]] = value.T
        matrix[across[0], across[1]] = value
        squares = squares + (1.0 if a == b else 2.0) * jnp.sum(value * value, keepdims=True)

    scaling = 2.5 * lax.rsqrt(squares)
    start = jnp.sqrt(jnp.sqrt(scaling))

    def factors_of(corner, first, last):
        identity = diagonal(half, 0, half)
        return [-0.25 * corner] + [
            jnp.where(identity, 1.25 - 0.25 * block, -0.25 * block) for block in (first, last)
        ]

    scaled = [
        matrix[rows, columns] * scaling
        for rows, columns in ((top, bottom), (top, top), (bottom, bottom))
    ]
    current.put_symmetric(strips, *scaled)
    scaled = factors_of(*scaled)
    factor.put_symmetric(strips, *scaled)
    result.put_symmetric(strips, *[start * block for block in scaled])

    def spread_terms():
        @pl.loop(0, blocks)
        def _(index):
            @pl.when(jnp.logical_not(jnp.logical_and(own_band, index == dp)))
            def _():
                from_server(index).wait_recv()

        terms_in[blocks] = jnp.zeros(terms_in.shape[1:], jnp.int16)
        owners = [owner_ref[served * blocks + index] for index in range(blocks)]

        @pl.loop(0, experts)
        def _(owner):
            at = jnp.int32(blocks)
            for index in range(blocks):
                at = jnp.where(owners[index] == owner, index, at)
            terms_out[owner] = terms_in[at]

        @pl.loop(1, experts)
        def _(step):
            to_owner(lax.rem(spot + step, experts)).start()

        owner_terms[slot, band] = terms_out[spot]

    def to_owner(other):
        return remote(
            terms_out.at[other],
            owner_terms.at[slot, band],
            spread_send.at[other],
            spread_recv.at[spot],
            dp,
            other,
        )

    def from_owner(other):
        return remote(
            terms_out.at[other],
            owner_terms.at[lax.rem(other, 2), other // 2],
            spread_send.at[other],
            spread_recv.at[other],
            dp,
            other,
        )

    for repeat in range(ITERS - 1):
        squared = symmetric_product(factor, factor, strips)
        if repeat > 0:
            advanced = symmetric_product(result, factor, strips)
        square.put_symmetric(strips, *squared)
        fourth = symmetric_product(square, square, strips)
        if repeat > 0:
            result.put_symmetric(strips, *advanced)
        factor.put_symmetric(strips, *fourth)
        following = symmetric_product(factor, current, strips)
        current.put_symmetric(strips, *following)
        factor.put_symmetric(strips, *factors_of(*following))
        if repeat == 3:
            spread_terms()
    result.put_symmetric(strips, *symmetric_product(result, factor, strips))

    width = extent // blocks
    inner = tiles * width

    def to_replica(index):
        return remote(
            band_codes.at[index],
            codes_out.at[dp],
            band_send.at[index],
            band_recv.at[dp],
            index,
            spot,
        )

    def from_replica(index):
        return remote(
            band_codes.at[index],
            codes_out.at[index],
            band_send.at[index],
            band_recv.at[index],
            index,
            spot,
        )

    keep = pltpu.make_async_copy(band_codes.at[dp], codes_out.at[dp], out_sem)
    for rows in strips:
        value = product(result, grad, rows, whole)
        for index in range(rows.start // width, (rows.start + rows.size) // width):
            first = index * width - rows.start
            note = jnp.zeros((NOTE, TILE), F32)
            for tile in range(tiles):
                codes, level = coded(value[first : first + width, tile * TILE : (tile + 1) * TILE])
                band_codes[index, tile * width : (tile + 1) * width, :] = codes
                note = jnp.where(line == tile, level, note)
            band_codes[index, inner:, :] = as_note(note, NOTE)

            @pl.when(index != dp)
            def _():
                to_replica(index).start()

            @pl.when(index == dp)
            def _():
                keep.start()

    @pl.loop(1, experts)
    def _(step):
        from_owner(lax.rem(spot + step, experts)).wait_recv()

    stores = []
    for where in range(2):
        for index in range(blocks):
            packed[where, index * depth : (index + 1) * depth, :] = decoded(
                owner_terms.at[where, index], depth
            )
        for place, (a, b) in enumerate(upper):
            value = GAIN / extent * packed[where, place * TILE : (place + 1) * TILE, :]
            down, over = pl.ds(a * TILE, TILE), pl.ds(b * TILE, TILE)
            fresh[where, down, over] = DECAY * previous[where, down, over] + value
            if a != b:
                fresh[where, over, down] = DECAY * previous[where, over, down] + value.T
        stores.append(pltpu.make_async_copy(fresh.at[where], fresh_out.at[where], load_sem.at[where]))
        stores[-1].start()

    for copy in crossing.values():
        copy.wait_send()
    for copy in (far_right, far_left, direct_right, direct_left, mixed_right, mixed_left):
        copy.wait_send()

    @pl.loop(1, experts)
    def _(step):
        other = lax.rem(spot + step, experts)
        to_plane(other).wait_send()
        to_owner(other).wait_send()

    @pl.loop(0, blocks)
    def _(index):
        @pl.when(jnp.logical_not(jnp.logical_and(own_band, index == dp)))
        def _():
            to_home(index).wait_send()
            to_server(index).wait_send()

    @pl.loop(1, blocks)
    def _(step):
        other = lax.rem(dp + step, blocks)
        to_replica(other).wait_send()
        from_replica(other).wait_recv()

    keep.wait()
    for copy in stores:
        copy.wait()


def finish(codes, fresh_in, fresh_out, precond_out, taken, passing, precond, load_sem, store_sem):
    load_codes = pltpu.make_async_copy(codes, taken, load_sem.at[2])
    load_codes.start()
    loads = [
        pltpu.make_async_copy(fresh_in.at[where], passing.at[where], load_sem.at[where])
        for where in range(2)
    ]
    for load in loads:
        load.start()
    blocks, width, extent = precond.shape
    tiles = extent // TILE
    inner = tiles * width
    stores = []
    load_codes.wait()
    for part in range(2):
        for index in range(part * blocks // 2, (part + 1) * blocks // 2):
            levels = floats(taken[index, inner:, :])
            for tile in range(tiles):
                line = tile * (NOTE // tiles)
                precond[index, :, tile * TILE : (tile + 1) * TILE] = floats(
                    taken[index, tile * width : (tile + 1) * width, :]
                ) * step_of(levels[line : line + 1, :])
        here = pl.ds(part * blocks // 2, blocks // 2)
        stores.append(
            pltpu.make_async_copy(precond.at[here], precond_out.at[here], store_sem.at[2 + part])
        )
        stores[-1].start()
        loads[part].wait()
        stores.append(
            pltpu.make_async_copy(passing.at[part], fresh_out.at[part], store_sem.at[part])
        )
        stores[-1].start()
    for store in stores:
        store.wait()


def per_device(grad_parts, stat_owned, owner_list):
    experts = lax.axis_size("expert")
    blocks = lax.axis_size("dp")
    partials, previous = grad_parts[0], stat_owned[0]
    extent = partials.shape[1]
    tiles = extent // TILE
    packed_rows = tiles * (tiles + 1) // 2 * TILE
    depth = packed_rows // blocks
    half = extent // 2
    dma = pltpu.SemaphoreType.DMA
    square = (extent, extent)
    width = extent // blocks
    inner = tiles * width + NOTE
    piece = (depth + NOTE, TILE)
    message = tiles * (half + half // 2) + NOTE
    terms, codes = pl.pallas_call(
        functools.partial(kernel, extent, blocks, experts),
        out_shape=[
            jax.ShapeDtypeStruct(previous.shape, F32),
            jax.ShapeDtypeStruct((blocks, inner, TILE), jnp.int16),
        ],
        in_specs=[pl.BlockSpec(memory_space=pl.ANY)] * 3,
        out_specs=[pl.BlockSpec(memory_space=pl.ANY)] * 2,
        scratch_shapes=[
            pltpu.SMEM(owner_list.shape, jnp.int32),
            pltpu.VMEM((RING, *square), BF16),
            pltpu.VMEM((RING, *square), BF16),
            pltpu.VMEM(square, F32),
            pltpu.VMEM((6, message, TILE), jnp.int16),
            pltpu.VMEM((6, message, TILE), jnp.int16),
            pltpu.VMEM((2, *square), F32),
            pltpu.VMEM((2, *square), F32),
            pltpu.VMEM((2, packed_rows, TILE), F32),
            pltpu.VMEM((2, blocks, *piece), jnp.int16),
            pltpu.VMEM((experts, *piece), jnp.int16),
            pltpu.VMEM((blocks, *piece), jnp.int16),
            pltpu.VMEM((blocks, *piece), jnp.int16),
            pltpu.VMEM((packed_rows, TILE), F32),
            pltpu.VMEM((blocks, *piece), jnp.int16),
            pltpu.VMEM((blocks + 1, *piece), jnp.int16),
            pltpu.VMEM((experts, *piece), jnp.int16),
            pltpu.VMEM((2, blocks, *piece), jnp.int16),
            pltpu.VMEM(square, F32),
            pltpu.VMEM((10, *square), BF16),
            pltpu.VMEM((blocks, inner, TILE), jnp.int16),
            dma((RING,)),
            dma(()),
            dma(()),
            pltpu.SemaphoreType.REGULAR,
            pltpu.SemaphoreType.REGULAR,
            dma((RING,)),
            dma((RING,)),
            dma((6,)),
            dma((6,)),
            dma((experts,)),
            dma((experts,)),
            dma((blocks,)),
            dma((blocks,)),
            dma((blocks,)),
            dma((blocks,)),
            dma((experts,)),
            dma((experts,)),
            dma((blocks,)),
            dma((blocks,)),
            dma(()),
        ],
        compiler_params=pltpu.CompilerParams(
            collective_id=0, has_side_effects=True, vmem_limit_bytes=60 * 2**20
        ),
    )(owner_list, partials, previous)
    fresh, precond = pl.pallas_call(
        finish,
        out_shape=[
            jax.ShapeDtypeStruct(previous.shape, F32),
            jax.ShapeDtypeStruct((blocks, width, extent), F32),
        ],
        in_specs=[pl.BlockSpec(memory_space=pl.ANY)] * 2,
        out_specs=[pl.BlockSpec(memory_space=pl.ANY)] * 2,
        scratch_shapes=[
            pltpu.VMEM(codes.shape, jnp.int16),
            pltpu.VMEM(previous.shape, F32),
            pltpu.VMEM((blocks, width, extent), F32),
            dma((3,)),
            dma((4,)),
        ],
        compiler_params=pltpu.CompilerParams(vmem_limit_bytes=60 * 2**20),
    )(codes, terms)
    return (fresh[None], precond)


def solution(mesh):
    in_specs = (P("dp", "expert", None, None), P("expert", "dp", None, None), P())
    out_specs = (P("expert", "dp", None, None), P("expert", "dp", None))
    return jax.shard_map(
        per_device, mesh=mesh, in_specs=in_specs, out_specs=out_specs, check_vma=False
    )
```

```python
import functools

import jax
import jax.numpy as jnp
from jax import lax
from jax.experimental import pallas as pl
from jax.experimental.pallas import tpu as pltpu
from jax.sharding import PartitionSpec as P

ITERS = 6
EPSILON = 1e-06
DECAY = 0.9
GAIN = 0.1

MESH = pl.DeviceIdType.MESH
F32 = jnp.float32
BF16 = jnp.bfloat16
TILE = 128
RING = 4
CORES = 2
LEVELS = 16.0
LOWEST = -1600.0
PEAK = 32700.0
NOTE = 16
WIDE = 22.0
BYTE = 256
HALFWAY = 32768


def remote(src, dst, send_sem, recv_sem, dp, expert):
    return pltpu.make_async_remote_copy(
        src_ref=src,
        dst_ref=dst,
        send_sem=send_sem,
        recv_sem=recv_sem,
        device_id={"dp": dp, "expert": expert},
        device_id_type=MESH,
    )


def split(value):
    high = value.astype(BF16)
    return high, (value - high.astype(F32)).astype(BF16)


def coded(value):
    peak = jnp.maximum(jnp.max(jnp.abs(value), axis=0, keepdims=True), 1e-30)
    level = jnp.maximum(jnp.ceil(LEVELS * jnp.log2(peak)), LOWEST)
    codes = jnp.round(value * (PEAK * jnp.exp2(level * (-1.0 / LEVELS))))
    return codes.astype(jnp.int32).astype(jnp.int16), level


def step_of(level):
    return jnp.exp2(level * (1.0 / LEVELS)) * (1.0 / PEAK)


def as_note(level, rows):
    return jnp.broadcast_to(level, (rows, level.shape[1])).astype(jnp.int32).astype(jnp.int16)


def floats(codes):
    return codes.astype(jnp.int32).astype(F32)


def pieces_of(tiles):
    above = [(a, b) for a in range(tiles) for b in range(a + 1, tiles)]
    return above, [(a, a + 1) for a in range(0, tiles, 2)]


def places():
    down = lax.broadcasted_iota(jnp.int32, (TILE, TILE), 0)
    over = lax.broadcasted_iota(jnp.int32, (TILE, TILE), 1)
    return down, over


def put_piece(piece, value, spine=None):
    codes, level = coded(value)
    piece[:TILE, :] = codes
    line = lax.broadcasted_iota(jnp.int32, (NOTE, TILE), 0)
    note = jnp.where(line < NOTE // 2, level, 0.0)
    if spine is not None:
        peak = jnp.maximum(jnp.max(jnp.abs(spine), axis=1, keepdims=True), 1e-30)
        level = jnp.maximum(jnp.ceil(LEVELS * jnp.log2(peak)), LOWEST)
        codes = jnp.round(spine * (PEAK * jnp.exp2(level * (-1.0 / LEVELS))))
        note = jnp.where(line < NOTE // 2, note, jnp.where(line < 3 * NOTE // 4, codes, level))
    piece[TILE:, :] = note.astype(jnp.int32).astype(jnp.int16)


def put_pieces(matrix, tile_of, tiles, after):
    above, paired = pieces_of(tiles)
    down, over = places()
    for index, (a, b) in enumerate(above):
        put_piece(matrix.at[index], tile_of(a, b))
        after(index)
    for index, (a, b) in enumerate(paired, len(above)):
        first = tile_of(a, a)
        spine = jnp.sum(jnp.where(down == over, first, 0.0), axis=0, keepdims=True)
        put_piece(matrix.at[index], jnp.where(down < over, first, tile_of(b, b)), spine)
        after(index)


def piece_value(piece):
    level = floats(piece[TILE:, :])[:1, :]
    return floats(piece[:TILE, :]) * step_of(level)


def diagonal_tiles(piece):
    value = piece_value(piece)
    note = floats(piece[TILE:, :])
    spine = note[NOTE // 2 : NOTE // 2 + 1, :] * step_of(note[NOTE - 1 :, :])
    down, over = places()
    across = value.T
    first = jnp.where(down < over, value, jnp.where(down == over, spine, across))
    return first, jnp.where(down < over, across, value)


def wide_coded(piece, tile, value):
    rows = value.shape[0]
    peak = jnp.maximum(jnp.max(jnp.abs(value), axis=0, keepdims=True), 1e-30)
    level = jnp.ceil(jnp.log2(peak))
    codes = jnp.round(value * jnp.exp2(WIDE - level)).astype(jnp.int32)
    first = tile * (rows + rows // 2)
    piece[first : first + rows, :] = (codes >> 8).astype(jnp.int16)
    low = codes & (BYTE - 1)
    low = low[: rows // 2, :] + (low[rows // 2 :, :] << 8) - HALFWAY
    piece[first + rows : first + rows + rows // 2, :] = low.astype(jnp.int16)
    return level


def wide_decoded(piece, tile, rows, tiles):
    first = tile * (rows + rows // 2)
    note = tiles * (rows + rows // 2)
    line = tile * (NOTE // tiles)
    level = floats(piece[note : note + NOTE, :])[line : line + 1, :]
    low = piece[first + rows : first + rows + rows // 2, :].astype(jnp.int32) + HALFWAY
    low = jnp.concatenate([low & (BYTE - 1), low >> 8], axis=0)
    codes = (piece[first : first + rows, :].astype(jnp.int32) << 8) + low
    return codes.astype(F32) * jnp.exp2(level - WIDE)


def dot(former, latter):
    return jnp.dot(former, latter, preferred_element_type=F32)


def dot_transposed(former, latter):
    return lax.dot_general(former, latter, (((1,), (1,)), ((), ())), preferred_element_type=F32)


def diagonal(rows, first, columns):
    across = lax.broadcasted_iota(jnp.int32, (rows, columns), 1)
    return lax.broadcasted_iota(jnp.int32, (rows, columns), 0) + first == across


class Pair:
    def __init__(self, high, low):
        self.high, self.low = high, low

    def put(self, rows, columns, value):
        self.high[rows, columns], self.low[rows, columns] = split(value)

    def put_symmetric(self, halves, corner, first, last):
        top, bottom = halves
        high, low = split(corner)
        self.high[top, bottom], self.low[top, bottom] = high, low
        self.high[bottom, top], self.low[bottom, top] = high.T, low.T
        self.put(top, top, first)
        self.put(bottom, bottom, last)


def product(former, latter, rows, columns, multiply=dot):
    def side(ref):
        return ref[:, columns] if multiply is dot else ref[columns, :]

    return multiply(former.high[rows, :], side(latter.high)) + (
        multiply(former.high[rows, :], side(latter.low))
        + multiply(former.low[rows, :], side(latter.high))
    )


def symmetric_product(former, latter, halves, multiply=dot):
    top, bottom = halves
    return [
        product(former, latter, rows, columns, multiply)
        for rows, columns in ((top, bottom), (top, top), (bottom, bottom))
    ]


def kernel(
    extent,
    blocks,
    experts,
    owner_list,
    grads,
    stats,
    owner_terms,
    codes_out,
    owner_ref,
    own,
    part,
    total,
    sent,
    received,
    previous,
    stat_codes,
    gathered,
    chosen,
    home_stat,
    term_codes,
    terms_in,
    terms_out,
    matrix,
    halves,
    band_codes,
    load_sem,
    stat_sem,
    owner_sem,
    ready_sem,
    open_sem,
    core_send,
    core_recv,
    ring_send,
    ring_recv,
    plane_send,
    plane_recv,
    home_send,
    home_recv,
    back_send,
    back_recv,
    spread_send,
    spread_recv,
    band_send,
    band_recv,
    out_sem,
    own_sem,
):
    dp = lax.axis_index("dp")
    spot = lax.axis_index("expert")
    x, core = dp // CORES, dp % CORES
    twin = x * CORES + 1 - core
    right = lax.rem(x + 1, RING) * CORES + core
    left = lax.rem(x + RING - 1, RING) * CORES + core
    slot, band = lax.rem(spot, 2), spot // 2
    served = 2 * dp + slot
    own_band = band == dp
    tiles = extent // TILE
    above, paired = pieces_of(tiles)
    half = extent // 2

    def block_of(turn, which):
        return lax.rem(x + turn, RING) * CORES + which

    loads = {}
    for turn in (2, 1, 3, 0):
        loads[turn] = pltpu.make_async_copy(
            grads.at[block_of(turn, core)], own.at[turn], load_sem.at[turn]
        )
        loads[turn].start()
    stat_load = pltpu.make_async_copy(stats, previous, stat_sem)
    stat_load.start()
    owner_load = pltpu.make_async_copy(owner_list, owner_ref, owner_sem)
    owner_load.start()

    barrier = pltpu.get_barrier_semaphore()
    gate = dp == 0

    def tell(semaphore, to_dp, to_expert):
        pl.semaphore_signal(
            semaphore, inc=1, device_id={"dp": to_dp, "expert": to_expert}, device_id_type=MESH
        )

    @pl.loop(1, blocks)
    def _(step):
        other = lax.rem(dp + step, blocks)

        @pl.when(other != 0)
        def _():
            tell(barrier, other, spot)

    def tile_at(index):
        return slice(index * TILE, (index + 1) * TILE)

    stat_load.wait()
    for where in range(2):
        put_pieces(
            stat_codes.at[where],
            lambda a, b, where=where: previous[where, tile_at(a), tile_at(b)],
            tiles,
            lambda index: None,
        )

    @pl.when(jnp.logical_not(gate))
    def _():
        pl.semaphore_wait(barrier, blocks - 1)
        tell(ready_sem, 0, spot)

    @pl.when(gate)
    def _():
        pl.semaphore_wait(ready_sem, blocks - 1)

        @pl.loop(1, experts)
        def _(step):
            tell(barrier, 0, lax.rem(spot + step, experts))

    crossing = {}
    for turn in (2, 1, 3, 0):
        crossing[turn] = remote(
            grads.at[block_of(turn, 1 - core)],
            part.at[turn],
            core_send.at[turn],
            core_recv.at[turn],
            twin,
            spot,
        )
        crossing[turn].start()

    def pair_sum(turn, rows, columns):
        return own[turn, rows, columns].astype(F32) + part[turn, rows, columns].astype(F32)

    top, bottom = pl.ds(0, half), pl.ds(half, half)
    line = lax.broadcasted_iota(jnp.int32, (NOTE, TILE), 0) // (NOTE // tiles)

    def ring(index, to):
        return remote(
            sent.at[index], received.at[index], ring_send.at[index], ring_recv.at[index], to, spot
        )

    def pass_on(index, to, turn, rows, arrived=None):
        note = jnp.zeros((NOTE, TILE), F32)
        for tile in range(tiles):
            value = pair_sum(turn, rows, pl.ds(tile * TILE, TILE))
            if arrived is not None:
                value = value + wide_decoded(received.at[arrived], tile, half, tiles)
            note = jnp.where(line == tile, wide_coded(sent.at[index], tile, value), note)
        sent[index, tiles * (half + half // 2) :, :] = as_note(note, NOTE)
        copy = ring(index, to)
        copy.start()
        return copy

    loads[2].wait()
    crossing[2].wait_recv()
    far_right = pass_on(0, right, 2, top)
    far_left = pass_on(1, left, 2, bottom)
    loads[1].wait()
    crossing[1].wait_recv()
    direct_right = pass_on(2, right, 1, bottom)
    loads[3].wait()
    crossing[3].wait_recv()
    direct_left = pass_on(3, left, 3, top)

    def to_plane(other):
        return remote(
            stat_codes.at[lax.rem(other, 2), other // 2],
            gathered.at[spot],
            plane_send.at[other],
            plane_recv.at[spot],
            dp,
            other,
        )

    def from_plane(other):
        return remote(
            stat_codes.at[0, 0], gathered.at[other], plane_send.at[other], plane_recv.at[other], dp, other
        )

    @pl.when(gate)
    def _():
        pl.semaphore_wait(barrier, experts - 1)

        @pl.loop(1, blocks)
        def _(step):
            tell(open_sem, step, spot)

    @pl.when(jnp.logical_not(gate))
    def _():
        pl.semaphore_wait(open_sem, 1)

    @pl.loop(1, experts)
    def _(step):
        to_plane(lax.rem(spot + step, experts)).start()

    gathered[spot] = stat_codes[slot, band]

    loads[0].wait()
    crossing[0].wait_recv()
    for rows in (top, bottom):
        total[rows, :] = pair_sum(0, rows, pl.ds(0, extent))

    far_right.wait_recv()
    mixed_right = pass_on(4, right, 1, top, 0)
    far_left.wait_recv()
    mixed_left = pass_on(5, left, 3, bottom, 1)

    @pl.loop(1, experts)
    def _(step):
        from_plane(lax.rem(spot + step, experts)).wait_recv()

    def to_home(index):
        return remote(
            chosen.at[index],
            home_stat.at[band],
            home_send.at[index],
            home_recv.at[band],
            index,
            served,
        )

    def from_home(index):
        return remote(
            chosen.at[index],
            home_stat.at[index],
            home_send.at[index],
            home_recv.at[index],
            band,
            2 * index + slot,
        )

    owner_load.wait()
    for index in range(blocks):
        mine = jnp.logical_and(own_band, dp == index)
        chosen[index] = gathered[owner_ref[served * blocks + index]]

        @pl.when(jnp.logical_not(mine))
        def _(index=index):
            to_home(index).start()

        @pl.when(mine)
        def _(index=index):
            home_stat[index] = chosen[index]

    for copy, index, rows in (
        (direct_left, 3, top),
        (direct_right, 2, bottom),
        (mixed_right, 4, top),
        (mixed_left, 5, bottom),
    ):
        copy.wait_recv()
        for tile in range(tiles):
            columns = pl.ds(tile * TILE, TILE)
            total[rows, columns] = total[rows, columns] + wide_decoded(
                received.at[index], tile, half, tiles
            )

    grad, current, factor, result, square = (
        Pair(halves.at[2 * index], halves.at[2 * index + 1]) for index in range(5)
    )
    strips = [top, bottom]
    whole = pl.ds(0, extent)
    for rows in strips:
        grad.put(rows, whole, total[rows, :])
    corner, first, last = symmetric_product(grad, grad, strips, dot_transposed)
    matrix[top, bottom] = corner
    matrix[top, top] = first
    matrix[bottom, bottom] = last
    def to_server(index):
        return remote(
            term_codes.at[index],
            terms_in.at[dp],
            back_send.at[index],
            back_recv.at[dp],
            band,
            2 * index + slot,
        )

    def from_server(index):
        return remote(
            term_codes.at[index],
            terms_in.at[index],
            back_send.at[index],
            back_recv.at[index],
            index,
            served,
        )

    def send_term(index):
        mine = jnp.logical_and(own_band, dp == index)

        @pl.when(jnp.logical_not(mine))
        def _():
            to_server(index).start()

        @pl.when(mine)
        def _():
            terms_in[index] = term_codes[index]

    put_pieces(term_codes, lambda a, b: matrix[tile_at(a), tile_at(b)], tiles, send_term)

    @pl.loop(0, blocks)
    def _(index):
        @pl.when(jnp.logical_not(jnp.logical_and(own_band, index == dp)))
        def _():
            from_home(index).wait_recv()

    squares = jnp.zeros((1, 1), F32)
    damping = jnp.where(diagonal(TILE, 0, TILE), F32(EPSILON), F32(0.0))
    for index, (a, b) in enumerate(above):
        value = DECAY * piece_value(home_stat.at[index]) + GAIN / extent * matrix[tile_at(a), tile_at(b)]
        matrix[tile_at(a), tile_at(b)] = value
        if a // (tiles // 2) == b // (tiles // 2):
            matrix[tile_at(b), tile_at(a)] = value.T
        squares = squares + 2.0 * jnp.sum(value * value, keepdims=True)
    for index, pair in enumerate(paired, len(above)):
        for a, value in zip(pair, diagonal_tiles(home_stat.at[index])):
            value = DECAY * value + GAIN / extent * matrix[tile_at(a), tile_at(a)] + damping
            matrix[tile_at(a), tile_at(a)] = value
            squares = squares + jnp.sum(value * value, keepdims=True)

    scaling = 2.5 * lax.rsqrt(squares)
    start = jnp.sqrt(jnp.sqrt(scaling))

    def factors_of(corner, first, last):
        identity = diagonal(half, 0, half)
        return [-0.25 * corner] + [
            jnp.where(identity, 1.25 - 0.25 * block, -0.25 * block) for block in (first, last)
        ]

    scaled = [
        matrix[rows, columns] * scaling
        for rows, columns in ((top, bottom), (top, top), (bottom, bottom))
    ]
    current.put_symmetric(strips, *scaled)
    scaled = factors_of(*scaled)
    factor.put_symmetric(strips, *scaled)
    result.put_symmetric(strips, *[start * block for block in scaled])

    keep_term = pltpu.make_async_copy(terms_out.at[spot], owner_terms.at[slot, band], own_sem)

    def spread_terms():
        @pl.loop(0, blocks)
        def _(index):
            @pl.when(jnp.logical_not(jnp.logical_and(own_band, index == dp)))
            def _():
                from_server(index).wait_recv()

        terms_in[blocks] = jnp.zeros(terms_in.shape[1:], jnp.int16)
        owners = [owner_ref[served * blocks + index] for index in range(blocks)]

        def spread_to(owner):
            at = jnp.int32(blocks)
            for index in range(blocks):
                at = jnp.where(owners[index] == owner, index, at)
            terms_out[owner] = terms_in[at]

        @pl.loop(1, experts)
        def _(step):
            other = lax.rem(spot + step, experts)
            spread_to(other)
            to_owner(other).start()

        spread_to(spot)
        keep_term.start()

    def to_owner(other):
        return remote(
            terms_out.at[other],
            owner_terms.at[slot, band],
            spread_send.at[other],
            spread_recv.at[spot],
            dp,
            other,
        )

    def from_owner(other):
        return remote(
            terms_out.at[other],
            owner_terms.at[lax.rem(other, 2), other // 2],
            spread_send.at[other],
            spread_recv.at[other],
            dp,
            other,
        )

    for repeat in range(ITERS - 1):
        squared = symmetric_product(factor, factor, strips)
        if repeat > 0:
            advanced = symmetric_product(result, factor, strips)
        square.put_symmetric(strips, *squared)
        fourth = symmetric_product(square, square, strips)
        if repeat > 0:
            result.put_symmetric(strips, *advanced)
        factor.put_symmetric(strips, *fourth)
        following = symmetric_product(factor, current, strips)
        current.put_symmetric(strips, *following)
        factor.put_symmetric(strips, *factors_of(*following))
        if repeat == 3:
            spread_terms()
    result.put_symmetric(strips, *symmetric_product(result, factor, strips))

    width = extent // blocks
    inner = tiles * width

    def to_replica(index):
        return remote(
            band_codes.at[index],
            codes_out.at[dp],
            band_send.at[index],
            band_recv.at[dp],
            index,
            spot,
        )

    def from_replica(index):
        return remote(
            band_codes.at[index],
            codes_out.at[index],
            band_send.at[index],
            band_recv.at[index],
            index,
            spot,
        )

    keep = pltpu.make_async_copy(band_codes.at[dp], codes_out.at[dp], out_sem)
    for rows in strips:
        value = product(result, grad, rows, whole)
        for index in range(rows.start // width, (rows.start + rows.size) // width):
            first = index * width - rows.start
            note = jnp.zeros((NOTE, TILE), F32)
            for tile in range(tiles):
                codes, level = coded(value[first : first + width, tile * TILE : (tile + 1) * TILE])
                band_codes[index, tile * width : (tile + 1) * width, :] = codes
                note = jnp.where(line == tile, level, note)
            band_codes[index, inner:, :] = as_note(note, NOTE)

            @pl.when(index != dp)
            def _():
                to_replica(index).start()

            @pl.when(index == dp)
            def _():
                keep.start()

    @pl.loop(1, experts)
    def _(step):
        from_owner(lax.rem(spot + step, experts)).wait_recv()

    for copy in crossing.values():
        copy.wait_send()
    for copy in (far_right, far_left, direct_right, direct_left, mixed_right, mixed_left):
        copy.wait_send()

    @pl.loop(1, experts)
    def _(step):
        other = lax.rem(spot + step, experts)
        to_plane(other).wait_send()
        to_owner(other).wait_send()

    @pl.loop(0, blocks)
    def _(index):
        @pl.when(jnp.logical_not(jnp.logical_and(own_band, index == dp)))
        def _():
            to_home(index).wait_send()
            to_server(index).wait_send()

    @pl.loop(1, blocks)
    def _(step):
        other = lax.rem(dp + step, blocks)
        to_replica(other).wait_send()
        from_replica(other).wait_recv()

    keep.wait()
    keep_term.wait()


def finish(
    codes,
    terms,
    stats,
    fresh_out,
    precond_out,
    taken,
    taken_terms,
    previous,
    precond,
    load_sem,
    store_sem,
):
    load_terms = pltpu.make_async_copy(terms, taken_terms, load_sem.at[3])
    load_terms.start()
    loads = [
        pltpu.make_async_copy(stats.at[where], previous.at[where], load_sem.at[where])
        for where in range(2)
    ]
    loads[0].start()
    load_codes = pltpu.make_async_copy(codes, taken, load_sem.at[2])
    load_codes.start()
    loads[1].start()
    blocks, width, extent = precond.shape
    tiles = extent // TILE
    inner = tiles * width
    above, paired = pieces_of(tiles)
    stores = []

    def store(src, dst, index):
        stores.append(pltpu.make_async_copy(src, dst, store_sem.at[index]))
        stores[-1].start()

    load_terms.wait()
    for part in range(2):
        loads[part].wait()

        def add(a, b, value, part=part):
            down, over = pl.ds(a * TILE, TILE), pl.ds(b * TILE, TILE)
            previous[part, down, over] = DECAY * previous[part, down, over] + GAIN / extent * value

        for index, (a, b) in enumerate(above):
            value = piece_value(taken_terms.at[part, index])
            add(a, b, value)
            add(b, a, value.T)
        for index, pair in enumerate(paired, len(above)):
            for a, value in zip(pair, diagonal_tiles(taken_terms.at[part, index])):
                add(a, a, value)
        store(previous.at[part], fresh_out.at[part], part)
        if part == 0:
            load_codes.wait()
        for index in range(part * blocks // 2, (part + 1) * blocks // 2):
            levels = floats(taken[index, inner:, :])
            for tile in range(tiles):
                line = tile * (NOTE // tiles)
                precond[index, :, tile * TILE : (tile + 1) * TILE] = floats(
                    taken[index, tile * width : (tile + 1) * width, :]
                ) * step_of(levels[line : line + 1, :])
        here = pl.ds(part * blocks // 2, blocks // 2)
        store(precond.at[here], precond_out.at[here], 2 + part)
    for copy in stores:
        copy.wait()


def per_device(grad_parts, stat_owned, owner_list):
    experts = lax.axis_size("expert")
    blocks = lax.axis_size("dp")
    partials, previous = grad_parts[0], stat_owned[0]
    extent = partials.shape[1]
    tiles = extent // TILE
    half = extent // 2
    dma = pltpu.SemaphoreType.DMA
    square = (extent, extent)
    width = extent // blocks
    inner = tiles * width + NOTE
    piece = (TILE + NOTE, TILE)
    message = tiles * (half + half // 2) + NOTE
    terms, codes = pl.pallas_call(
        functools.partial(kernel, extent, blocks, experts),
        out_shape=[
            jax.ShapeDtypeStruct((2, blocks, *piece), jnp.int16),
            jax.ShapeDtypeStruct((blocks, inner, TILE), jnp.int16),
        ],
        in_specs=[pl.BlockSpec(memory_space=pl.ANY)] * 3,
        out_specs=[pl.BlockSpec(memory_space=pl.ANY)] * 2,
        scratch_shapes=[
            pltpu.SMEM(owner_list.shape, jnp.int32),
            pltpu.VMEM((RING, *square), BF16),
            pltpu.VMEM((RING, *square), BF16),
            pltpu.VMEM(square, F32),
            pltpu.VMEM((6, message, TILE), jnp.int16),
            pltpu.VMEM((6, message, TILE), jnp.int16),
            pltpu.VMEM((2, *square), F32),
            pltpu.VMEM((2, blocks, *piece), jnp.int16),
            pltpu.VMEM((experts, *piece), jnp.int16),
            pltpu.VMEM((blocks, *piece), jnp.int16),
            pltpu.VMEM((blocks, *piece), jnp.int16),
            pltpu.VMEM((blocks, *piece), jnp.int16),
            pltpu.VMEM((blocks + 1, *piece), jnp.int16),
            pltpu.VMEM((experts, *piece), jnp.int16),
            pltpu.VMEM(square, F32),
            pltpu.VMEM((10, *square), BF16),
            pltpu.VMEM((blocks, inner, TILE), jnp.int16),
            dma((RING,)),
            dma(()),
            dma(()),
            pltpu.SemaphoreType.REGULAR,
            pltpu.SemaphoreType.REGULAR,
            dma((RING,)),
            dma((RING,)),
            dma((6,)),
            dma((6,)),
            dma((experts,)),
            dma((experts,)),
            dma((blocks,)),
            dma((blocks,)),
            dma((blocks,)),
            dma((blocks,)),
            dma((experts,)),
            dma((experts,)),
            dma((blocks,)),
            dma((blocks,)),
            dma(()),
            dma(()),
        ],
        compiler_params=pltpu.CompilerParams(
            collective_id=0, has_side_effects=True, vmem_limit_bytes=60 * 2**20
        ),
    )(owner_list, partials, previous)
    fresh, precond = pl.pallas_call(
        finish,
        out_shape=[
            jax.ShapeDtypeStruct(previous.shape, F32),
            jax.ShapeDtypeStruct((blocks, width, extent), F32),
        ],
        in_specs=[pl.BlockSpec(memory_space=pl.ANY)] * 3,
        out_specs=[pl.BlockSpec(memory_space=pl.ANY)] * 2,
        scratch_shapes=[
            pltpu.VMEM(codes.shape, jnp.int16),
            pltpu.VMEM(terms.shape, jnp.int16),
            pltpu.VMEM(previous.shape, F32),
            pltpu.VMEM((blocks, width, extent), F32),
            dma((4,)),
            dma((4,)),
        ],
        compiler_params=pltpu.CompilerParams(vmem_limit_bytes=60 * 2**20),
    )(codes, terms, previous)
    return (fresh[None], precond)


def solution(mesh):
    in_specs = (P("dp", "expert", None, None), P("expert", "dp", None, None), P())
    out_specs = (P("expert", "dp", None, None), P("expert", "dp", None))
    return jax.shard_map(
        per_device, mesh=mesh, in_specs=in_specs, out_specs=out_specs, check_vma=False
    )
```

```python
import functools

import jax
import jax.numpy as jnp
from jax import lax
from jax.experimental import pallas as pl
from jax.experimental.pallas import tpu as pltpu
from jax.sharding import PartitionSpec as P

ITERS = 6
EPSILON = 1e-06
DECAY = 0.9
GAIN = 0.1

MESH = pl.DeviceIdType.MESH
F32 = jnp.float32
BF16 = jnp.bfloat16
TILE = 128
RING = 4
CORES = 2
LEVELS = 16.0
LOWEST = -1600.0
PEAK = 32700.0
NOTE = 16
WIDE = 22.0
BYTE = 256
HALFWAY = 32768


def remote(src, dst, send_sem, recv_sem, dp, expert):
    return pltpu.make_async_remote_copy(
        src_ref=src,
        dst_ref=dst,
        send_sem=send_sem,
        recv_sem=recv_sem,
        device_id={"dp": dp, "expert": expert},
        device_id_type=MESH,
    )


def split(value):
    high = value.astype(BF16)
    return high, (value - high.astype(F32)).astype(BF16)


def coded(value):
    peak = jnp.maximum(jnp.max(jnp.abs(value), axis=0, keepdims=True), 1e-30)
    level = jnp.maximum(jnp.ceil(LEVELS * jnp.log2(peak)), LOWEST)
    codes = jnp.round(value * (PEAK * jnp.exp2(level * (-1.0 / LEVELS))))
    return codes.astype(jnp.int32).astype(jnp.int16), level


def step_of(level):
    return jnp.exp2(level * (1.0 / LEVELS)) * (1.0 / PEAK)


def as_note(level, rows):
    return jnp.broadcast_to(level, (rows, level.shape[1])).astype(jnp.int32).astype(jnp.int16)


def floats(codes):
    return codes.astype(jnp.int32).astype(F32)


def pieces_of(tiles):
    above = [(a, b) for a in range(tiles) for b in range(a + 1, tiles)]
    return above, [(a, a + 1) for a in range(0, tiles, 2)]


def places():
    down = lax.broadcasted_iota(jnp.int32, (TILE, TILE), 0)
    over = lax.broadcasted_iota(jnp.int32, (TILE, TILE), 1)
    return down, over


def put_piece(piece, value, spine=None):
    codes, level = coded(value)
    piece[:TILE, :] = codes
    line = lax.broadcasted_iota(jnp.int32, (NOTE, TILE), 0)
    note = jnp.where(line < NOTE // 2, level, 0.0)
    if spine is not None:
        peak = jnp.maximum(jnp.max(jnp.abs(spine), axis=1, keepdims=True), 1e-30)
        level = jnp.maximum(jnp.ceil(LEVELS * jnp.log2(peak)), LOWEST)
        codes = jnp.round(spine * (PEAK * jnp.exp2(level * (-1.0 / LEVELS))))
        note = jnp.where(line < NOTE // 2, note, jnp.where(line < 3 * NOTE // 4, codes, level))
    piece[TILE:, :] = note.astype(jnp.int32).astype(jnp.int16)


def put_pieces(matrix, tile_of, tiles, after):
    above, paired = pieces_of(tiles)
    down, over = places()
    for index, (a, b) in enumerate(above):
        put_piece(matrix.at[index], tile_of(a, b))
        after(index)
    for index, (a, b) in enumerate(paired, len(above)):
        first = tile_of(a, a)
        spine = jnp.sum(jnp.where(down == over, first, 0.0), axis=0, keepdims=True)
        put_piece(matrix.at[index], jnp.where(down < over, first, tile_of(b, b)), spine)
        after(index)


def piece_value(piece):
    level = floats(piece[TILE:, :])[:1, :]
    return floats(piece[:TILE, :]) * step_of(level)


def diagonal_tiles(piece):
    value = piece_value(piece)
    note = floats(piece[TILE:, :])
    spine = note[NOTE // 2 : NOTE // 2 + 1, :] * step_of(note[NOTE - 1 :, :])
    down, over = places()
    across = value.T
    first = jnp.where(down < over, value, jnp.where(down == over, spine, across))
    return first, jnp.where(down < over, across, value)


def wide_coded(piece, tile, value):
    rows = value.shape[0]
    peak = jnp.maximum(jnp.max(jnp.abs(value), axis=0, keepdims=True), 1e-30)
    level = jnp.ceil(jnp.log2(peak))
    codes = jnp.round(value * jnp.exp2(WIDE - level)).astype(jnp.int32)
    first = tile * (rows + rows // 2)
    piece[first : first + rows, :] = (codes >> 8).astype(jnp.int16)
    low = codes & (BYTE - 1)
    low = low[: rows // 2, :] + (low[rows // 2 :, :] << 8) - HALFWAY
    piece[first + rows : first + rows + rows // 2, :] = low.astype(jnp.int16)
    return level


def wide_decoded(piece, tile, rows, tiles):
    first = tile * (rows + rows // 2)
    note = tiles * (rows + rows // 2)
    line = tile * (NOTE // tiles)
    level = floats(piece[note : note + NOTE, :])[line : line + 1, :]
    low = piece[first + rows : first + rows + rows // 2, :].astype(jnp.int32) + HALFWAY
    low = jnp.concatenate([low & (BYTE - 1), low >> 8], axis=0)
    codes = (piece[first : first + rows, :].astype(jnp.int32) << 8) + low
    return codes.astype(F32) * jnp.exp2(level - WIDE)


def dot(former, latter):
    return jnp.dot(former, latter, preferred_element_type=F32)


def dot_transposed(former, latter):
    return lax.dot_general(former, latter, (((1,), (1,)), ((), ())), preferred_element_type=F32)


def diagonal(rows, first, columns):
    across = lax.broadcasted_iota(jnp.int32, (rows, columns), 1)
    return lax.broadcasted_iota(jnp.int32, (rows, columns), 0) + first == across


class Pair:
    def __init__(self, high, low):
        self.high, self.low = high, low

    def put(self, rows, columns, value):
        self.high[rows, columns], self.low[rows, columns] = split(value)

    def put_symmetric(self, halves, corner, first, last):
        top, bottom = halves
        high, low = split(corner)
        self.high[top, bottom], self.low[top, bottom] = high, low
        self.high[bottom, top], self.low[bottom, top] = high.T, low.T
        self.put(top, top, first)
        self.put(bottom, bottom, last)


def product(former, latter, rows, columns, multiply=dot):
    def side(ref):
        return ref[:, columns] if multiply is dot else ref[columns, :]

    return multiply(former.high[rows, :], side(latter.high)) + (
        multiply(former.high[rows, :], side(latter.low))
        + multiply(former.low[rows, :], side(latter.high))
    )


def symmetric_product(former, latter, halves, multiply=dot):
    top, bottom = halves
    return [
        product(former, latter, rows, columns, multiply)
        for rows, columns in ((top, bottom), (top, top), (bottom, bottom))
    ]


def kernel(
    extent,
    blocks,
    experts,
    owner_list,
    grads,
    stats,
    owner_terms,
    codes_out,
    owner_ref,
    own,
    part,
    total,
    sent,
    received,
    previous,
    stat_codes,
    gathered,
    chosen,
    home_stat,
    term_codes,
    terms_in,
    terms_out,
    matrix,
    halves,
    band_codes,
    load_sem,
    stat_sem,
    owner_sem,
    ready_sem,
    open_sem,
    core_send,
    core_recv,
    ring_send,
    ring_recv,
    plane_send,
    plane_recv,
    home_send,
    home_recv,
    back_send,
    back_recv,
    spread_send,
    spread_recv,
    band_send,
    band_recv,
    out_sem,
    own_sem,
):
    dp = lax.axis_index("dp")
    spot = lax.axis_index("expert")
    x, core = dp // CORES, dp % CORES
    twin = x * CORES + 1 - core
    right = lax.rem(x + 1, RING) * CORES + core
    left = lax.rem(x + RING - 1, RING) * CORES + core
    slot, band = lax.rem(spot, 2), spot // 2
    served = 2 * dp + slot
    own_band = band == dp
    tiles = extent // TILE
    above, paired = pieces_of(tiles)
    half = extent // 2

    def block_of(turn, which):
        return lax.rem(x + turn, RING) * CORES + which

    loads = {}
    for turn in (2, 1, 3, 0):
        loads[turn] = pltpu.make_async_copy(
            grads.at[block_of(turn, core)], own.at[turn], load_sem.at[turn]
        )
        loads[turn].start()
    stat_load = pltpu.make_async_copy(stats, previous, stat_sem)
    stat_load.start()
    owner_load = pltpu.make_async_copy(owner_list, owner_ref, owner_sem)
    owner_load.start()

    barrier = pltpu.get_barrier_semaphore()
    gate = dp == 0

    def tell(semaphore, to_dp, to_expert):
        pl.semaphore_signal(
            semaphore, inc=1, device_id={"dp": to_dp, "expert": to_expert}, device_id_type=MESH
        )

    @pl.loop(1, blocks)
    def _(step):
        other = lax.rem(dp + step, blocks)

        @pl.when(other != 0)
        def _():
            tell(barrier, other, spot)

    @pl.when(jnp.logical_not(gate))
    def _():
        pl.semaphore_wait(barrier, blocks - 1)
        tell(ready_sem, 0, spot)

    @pl.when(gate)
    def _():
        pl.semaphore_wait(ready_sem, blocks - 1)

        @pl.loop(1, experts)
        def _(step):
            tell(barrier, 0, lax.rem(spot + step, experts))

    crossing = {}
    for turn in (2, 1, 3, 0):
        crossing[turn] = remote(
            grads.at[block_of(turn, 1 - core)],
            part.at[turn],
            core_send.at[turn],
            core_recv.at[turn],
            twin,
            spot,
        )
        crossing[turn].start()

    def tile_at(index):
        return slice(index * TILE, (index + 1) * TILE)

    stat_load.wait()
    for where in range(2):
        put_pieces(
            stat_codes.at[where],
            lambda a, b, where=where: previous[where, tile_at(a), tile_at(b)],
            tiles,
            lambda index: None,
        )

    def pair_sum(turn, rows, columns):
        return own[turn, rows, columns].astype(F32) + part[turn, rows, columns].astype(F32)

    top, bottom = pl.ds(0, half), pl.ds(half, half)
    line = lax.broadcasted_iota(jnp.int32, (NOTE, TILE), 0) // (NOTE // tiles)

    def ring(index, to):
        return remote(
            sent.at[index], received.at[index], ring_send.at[index], ring_recv.at[index], to, spot
        )

    def pass_on(index, to, turn, rows, arrived=None):
        note = jnp.zeros((NOTE, TILE), F32)
        for tile in range(tiles):
            value = pair_sum(turn, rows, pl.ds(tile * TILE, TILE))
            if arrived is not None:
                value = value + wide_decoded(received.at[arrived], tile, half, tiles)
            note = jnp.where(line == tile, wide_coded(sent.at[index], tile, value), note)
        sent[index, tiles * (half + half // 2) :, :] = as_note(note, NOTE)
        copy = ring(index, to)
        copy.start()
        return copy

    loads[2].wait()
    crossing[2].wait_recv()
    far_right = pass_on(0, right, 2, top)
    far_left = pass_on(1, left, 2, bottom)
    loads[1].wait()
    crossing[1].wait_recv()
    direct_right = pass_on(2, right, 1, bottom)
    loads[3].wait()
    crossing[3].wait_recv()
    direct_left = pass_on(3, left, 3, top)

    def to_plane(other):
        return remote(
            stat_codes.at[lax.rem(other, 2), other // 2],
            gathered.at[spot],
            plane_send.at[other],
            plane_recv.at[spot],
            dp,
            other,
        )

    def from_plane(other):
        return remote(
            stat_codes.at[0, 0], gathered.at[other], plane_send.at[other], plane_recv.at[other], dp, other
        )

    @pl.when(gate)
    def _():
        pl.semaphore_wait(barrier, experts - 1)

        @pl.loop(1, blocks)
        def _(step):
            tell(open_sem, step, spot)

    @pl.when(jnp.logical_not(gate))
    def _():
        pl.semaphore_wait(open_sem, 1)

    @pl.loop(1, experts)
    def _(step):
        to_plane(lax.rem(spot + step, experts)).start()

    gathered[spot] = stat_codes[slot, band]

    loads[0].wait()
    crossing[0].wait_recv()
    for rows in (top, bottom):
        total[rows, :] = pair_sum(0, rows, pl.ds(0, extent))

    far_right.wait_recv()
    mixed_right = pass_on(4, right, 1, top, 0)
    far_left.wait_recv()
    mixed_left = pass_on(5, left, 3, bottom, 1)

    @pl.loop(1, experts)
    def _(step):
        from_plane(lax.rem(spot + step, experts)).wait_recv()

    def to_home(index):
        return remote(
            chosen.at[index],
            home_stat.at[band],
            home_send.at[index],
            home_recv.at[band],
            index,
            served,
        )

    def from_home(index):
        return remote(
            chosen.at[index],
            home_stat.at[index],
            home_send.at[index],
            home_recv.at[index],
            band,
            2 * index + slot,
        )

    owner_load.wait()
    for index in range(blocks):
        mine = jnp.logical_and(own_band, dp == index)
        chosen[index] = gathered[owner_ref[served * blocks + index]]

        @pl.when(jnp.logical_not(mine))
        def _(index=index):
            to_home(index).start()

        @pl.when(mine)
        def _(index=index):
            home_stat[index] = chosen[index]

    for copy, index, rows in (
        (direct_left, 3, top),
        (direct_right, 2, bottom),
        (mixed_right, 4, top),
        (mixed_left, 5, bottom),
    ):
        copy.wait_recv()
        for tile in range(tiles):
            columns = pl.ds(tile * TILE, TILE)
            total[rows, columns] = total[rows, columns] + wide_decoded(
                received.at[index], tile, half, tiles
            )

    grad, current, factor, result, square = (
        Pair(halves.at[2 * index], halves.at[2 * index + 1]) for index in range(5)
    )
    strips = [top, bottom]
    whole = pl.ds(0, extent)
    for rows in strips:
        grad.put(rows, whole, total[rows, :])
    corner, first, last = symmetric_product(grad, grad, strips, dot_transposed)
    matrix[top, bottom] = corner
    matrix[top, top] = first
    matrix[bottom, bottom] = last
    def to_server(index):
        return remote(
            term_codes.at[index],
            terms_in.at[dp],
            back_send.at[index],
            back_recv.at[dp],
            band,
            2 * index + slot,
        )

    def from_server(index):
        return remote(
            term_codes.at[index],
            terms_in.at[index],
            back_send.at[index],
            back_recv.at[index],
            index,
            served,
        )

    def send_term(index):
        mine = jnp.logical_and(own_band, dp == index)

        @pl.when(jnp.logical_not(mine))
        def _():
            to_server(index).start()

        @pl.when(mine)
        def _():
            terms_in[index] = term_codes[index]

    put_pieces(term_codes, lambda a, b: matrix[tile_at(a), tile_at(b)], tiles, send_term)

    @pl.loop(0, blocks)
    def _(index):
        @pl.when(jnp.logical_not(jnp.logical_and(own_band, index == dp)))
        def _():
            from_home(index).wait_recv()

    squares = jnp.zeros((1, 1), F32)
    damping = jnp.where(diagonal(TILE, 0, TILE), F32(EPSILON), F32(0.0))
    for index, (a, b) in enumerate(above):
        value = DECAY * piece_value(home_stat.at[index]) + GAIN / extent * matrix[tile_at(a), tile_at(b)]
        matrix[tile_at(a), tile_at(b)] = value
        if a // (tiles // 2) == b // (tiles // 2):
            matrix[tile_at(b), tile_at(a)] = value.T
        squares = squares + 2.0 * jnp.sum(value * value, keepdims=True)
    for index, pair in enumerate(paired, len(above)):
        for a, value in zip(pair, diagonal_tiles(home_stat.at[index])):
            value = DECAY * value + GAIN / extent * matrix[tile_at(a), tile_at(a)] + damping
            matrix[tile_at(a), tile_at(a)] = value
            squares = squares + jnp.sum(value * value, keepdims=True)

    scaling = 2.5 * lax.rsqrt(squares)
    start = jnp.sqrt(jnp.sqrt(scaling))

    def factors_of(corner, first, last):
        identity = diagonal(half, 0, half)
        return [-0.25 * corner] + [
            jnp.where(identity, 1.25 - 0.25 * block, -0.25 * block) for block in (first, last)
        ]

    scaled = [
        matrix[rows, columns] * scaling
        for rows, columns in ((top, bottom), (top, top), (bottom, bottom))
    ]
    current.put_symmetric(strips, *scaled)
    scaled = factors_of(*scaled)
    factor.put_symmetric(strips, *scaled)
    result.put_symmetric(strips, *[start * block for block in scaled])

    keep_term = pltpu.make_async_copy(terms_out.at[spot], owner_terms.at[slot, band], own_sem)

    def spread_terms():
        @pl.loop(0, blocks)
        def _(index):
            @pl.when(jnp.logical_not(jnp.logical_and(own_band, index == dp)))
            def _():
                from_server(index).wait_recv()

        terms_in[blocks] = jnp.zeros(terms_in.shape[1:], jnp.int16)
        owners = [owner_ref[served * blocks + index] for index in range(blocks)]

        def spread_to(owner):
            at = jnp.int32(blocks)
            for index in range(blocks):
                at = jnp.where(owners[index] == owner, index, at)
            terms_out[owner] = terms_in[at]

        @pl.loop(1, experts)
        def _(step):
            other = lax.rem(spot + step, experts)
            spread_to(other)
            to_owner(other).start()

        spread_to(spot)
        keep_term.start()

    def to_owner(other):
        return remote(
            terms_out.at[other],
            owner_terms.at[slot, band],
            spread_send.at[other],
            spread_recv.at[spot],
            dp,
            other,
        )

    def from_owner(other):
        return remote(
            terms_out.at[other],
            owner_terms.at[lax.rem(other, 2), other // 2],
            spread_send.at[other],
            spread_recv.at[other],
            dp,
            other,
        )

    for repeat in range(ITERS - 1):
        squared = symmetric_product(factor, factor, strips)
        if repeat > 0:
            advanced = symmetric_product(result, factor, strips)
        square.put_symmetric(strips, *squared)
        fourth = symmetric_product(square, square, strips)
        if repeat > 0:
            result.put_symmetric(strips, *advanced)
        factor.put_symmetric(strips, *fourth)
        following = symmetric_product(factor, current, strips)
        current.put_symmetric(strips, *following)
        factor.put_symmetric(strips, *factors_of(*following))
        if repeat == 3:
            spread_terms()
    result.put_symmetric(strips, *symmetric_product(result, factor, strips))

    width = extent // blocks
    inner = tiles * width

    def to_replica(index):
        return remote(
            band_codes.at[index],
            codes_out.at[dp],
            band_send.at[index],
            band_recv.at[dp],
            index,
            spot,
        )

    def from_replica(index):
        return remote(
            band_codes.at[index],
            codes_out.at[index],
            band_send.at[index],
            band_recv.at[index],
            index,
            spot,
        )

    keep = pltpu.make_async_copy(band_codes.at[dp], codes_out.at[dp], out_sem)
    for rows in strips:
        value = product(result, grad, rows, whole)
        for index in range(rows.start // width, (rows.start + rows.size) // width):
            first = index * width - rows.start
            note = jnp.zeros((NOTE, TILE), F32)
            for tile in range(tiles):
                codes, level = coded(value[first : first + width, tile * TILE : (tile + 1) * TILE])
                band_codes[index, tile * width : (tile + 1) * width, :] = codes
                note = jnp.where(line == tile, level, note)
            band_codes[index, inner:, :] = as_note(note, NOTE)

            @pl.when(index != dp)
            def _():
                to_replica(index).start()

            @pl.when(index == dp)
            def _():
                keep.start()

    @pl.loop(1, experts)
    def _(step):
        from_owner(lax.rem(spot + step, experts)).wait_recv()

    for copy in crossing.values():
        copy.wait_send()
    for copy in (far_right, far_left, direct_right, direct_left, mixed_right, mixed_left):
        copy.wait_send()

    @pl.loop(1, experts)
    def _(step):
        other = lax.rem(spot + step, experts)
        to_plane(other).wait_send()
        to_owner(other).wait_send()

    @pl.loop(0, blocks)
    def _(index):
        @pl.when(jnp.logical_not(jnp.logical_and(own_band, index == dp)))
        def _():
            to_home(index).wait_send()
            to_server(index).wait_send()

    @pl.loop(1, blocks)
    def _(step):
        other = lax.rem(dp + step, blocks)
        to_replica(other).wait_send()
        from_replica(other).wait_recv()

    keep.wait()
    keep_term.wait()


def finish(
    codes,
    terms,
    stats,
    fresh_out,
    precond_out,
    taken,
    taken_terms,
    previous,
    precond,
    load_sem,
    store_sem,
):
    load_terms = pltpu.make_async_copy(terms, taken_terms, load_sem.at[3])
    load_terms.start()
    loads = [
        pltpu.make_async_copy(stats.at[where], previous.at[where], load_sem.at[where])
        for where in range(2)
    ]
    loads[0].start()
    load_codes = pltpu.make_async_copy(codes, taken, load_sem.at[2])
    load_codes.start()
    loads[1].start()
    blocks, width, extent = precond.shape
    tiles = extent // TILE
    inner = tiles * width
    above, paired = pieces_of(tiles)
    stores = []

    def store(src, dst, index):
        stores.append(pltpu.make_async_copy(src, dst, store_sem.at[index]))
        stores[-1].start()

    load_terms.wait()
    for part in range(2):
        loads[part].wait()

        def add(a, b, value, part=part):
            down, over = pl.ds(a * TILE, TILE), pl.ds(b * TILE, TILE)
            previous[part, down, over] = DECAY * previous[part, down, over] + GAIN / extent * value

        for index, (a, b) in enumerate(above):
            value = piece_value(taken_terms.at[part, index])
            add(a, b, value)
            add(b, a, value.T)
        for index, pair in enumerate(paired, len(above)):
            for a, value in zip(pair, diagonal_tiles(taken_terms.at[part, index])):
                add(a, a, value)
        store(previous.at[part], fresh_out.at[part], part)
        if part == 0:
            load_codes.wait()
        for index in range(part * blocks // 2, (part + 1) * blocks // 2):
            levels = floats(taken[index, inner:, :])
            for tile in range(tiles):
                line = tile * (NOTE // tiles)
                precond[index, :, tile * TILE : (tile + 1) * TILE] = floats(
                    taken[index, tile * width : (tile + 1) * width, :]
                ) * step_of(levels[line : line + 1, :])
        here = pl.ds(part * blocks // 2, blocks // 2)
        store(precond.at[here], precond_out.at[here], 2 + part)
    for copy in stores:
        copy.wait()


def per_device(grad_parts, stat_owned, owner_list):
    experts = lax.axis_size("expert")
    blocks = lax.axis_size("dp")
    partials, previous = grad_parts[0], stat_owned[0]
    extent = partials.shape[1]
    tiles = extent // TILE
    half = extent // 2
    dma = pltpu.SemaphoreType.DMA
    square = (extent, extent)
    width = extent // blocks
    inner = tiles * width + NOTE
    piece = (TILE + NOTE, TILE)
    message = tiles * (half + half // 2) + NOTE
    terms, codes = pl.pallas_call(
        functools.partial(kernel, extent, blocks, experts),
        out_shape=[
            jax.ShapeDtypeStruct((2, blocks, *piece), jnp.int16),
            jax.ShapeDtypeStruct((blocks, inner, TILE), jnp.int16),
        ],
        in_specs=[pl.BlockSpec(memory_space=pl.ANY)] * 3,
        out_specs=[pl.BlockSpec(memory_space=pl.ANY)] * 2,
        scratch_shapes=[
            pltpu.SMEM(owner_list.shape, jnp.int32),
            pltpu.VMEM((RING, *square), BF16),
            pltpu.VMEM((RING, *square), BF16),
            pltpu.VMEM(square, F32),
            pltpu.VMEM((6, message, TILE), jnp.int16),
            pltpu.VMEM((6, message, TILE), jnp.int16),
            pltpu.VMEM((2, *square), F32),
            pltpu.VMEM((2, blocks, *piece), jnp.int16),
            pltpu.VMEM((experts, *piece), jnp.int16),
            pltpu.VMEM((blocks, *piece), jnp.int16),
            pltpu.VMEM((blocks, *piece), jnp.int16),
            pltpu.VMEM((blocks, *piece), jnp.int16),
            pltpu.VMEM((blocks + 1, *piece), jnp.int16),
            pltpu.VMEM((experts, *piece), jnp.int16),
            pltpu.VMEM(square, F32),
            pltpu.VMEM((10, *square), BF16),
            pltpu.VMEM((blocks, inner, TILE), jnp.int16),
            dma((RING,)),
            dma(()),
            dma(()),
            pltpu.SemaphoreType.REGULAR,
            pltpu.SemaphoreType.REGULAR,
            dma((RING,)),
            dma((RING,)),
            dma((6,)),
            dma((6,)),
            dma((experts,)),
            dma((experts,)),
            dma((blocks,)),
            dma((blocks,)),
            dma((blocks,)),
            dma((blocks,)),
            dma((experts,)),
            dma((experts,)),
            dma((blocks,)),
            dma((blocks,)),
            dma(()),
            dma(()),
        ],
        compiler_params=pltpu.CompilerParams(
            collective_id=0, has_side_effects=True, vmem_limit_bytes=60 * 2**20
        ),
    )(owner_list, partials, previous)
    fresh, precond = pl.pallas_call(
        finish,
        out_shape=[
            jax.ShapeDtypeStruct(previous.shape, F32),
            jax.ShapeDtypeStruct((blocks, width, extent), F32),
        ],
        in_specs=[pl.BlockSpec(memory_space=pl.ANY)] * 3,
        out_specs=[pl.BlockSpec(memory_space=pl.ANY)] * 2,
        scratch_shapes=[
            pltpu.VMEM(codes.shape, jnp.int16),
            pltpu.VMEM(terms.shape, jnp.int16),
            pltpu.VMEM(previous.shape, F32),
            pltpu.VMEM((blocks, width, extent), F32),
            dma((4,)),
            dma((4,)),
        ],
        compiler_params=pltpu.CompilerParams(vmem_limit_bytes=60 * 2**20),
    )(codes, terms, previous)
    return (fresh[None], precond)


def solution(mesh):
    in_specs = (P("dp", "expert", None, None), P("expert", "dp", None, None), P())
    out_specs = (P("expert", "dp", None, None), P("expert", "dp", None))
    return jax.shard_map(
        per_device, mesh=mesh, in_specs=in_specs, out_specs=out_specs, check_vma=False
    )
```

```python
import functools

import jax
import jax.numpy as jnp
from jax import lax
from jax.experimental import pallas as pl
from jax.experimental.pallas import tpu as pltpu
from jax.sharding import PartitionSpec as P

ITERS = 6
EPSILON = 1e-06
DECAY = 0.9
GAIN = 0.1

MESH = pl.DeviceIdType.MESH
F32 = jnp.float32
BF16 = jnp.bfloat16
TILE = 128
RING = 4
CORES = 2
LEVELS = 16.0
LOWEST = -1600.0
PEAK = 32700.0
NOTE = 16
WIDE = 22.0
BYTE = 256
HALFWAY = 32768


def remote(src, dst, send_sem, recv_sem, dp, expert):
    return pltpu.make_async_remote_copy(
        src_ref=src,
        dst_ref=dst,
        send_sem=send_sem,
        recv_sem=recv_sem,
        device_id={"dp": dp, "expert": expert},
        device_id_type=MESH,
    )


def split(value):
    high = value.astype(BF16)
    return high, (value - high.astype(F32)).astype(BF16)


def coded(value):
    peak = jnp.maximum(jnp.max(jnp.abs(value), axis=0, keepdims=True), 1e-30)
    level = jnp.maximum(jnp.ceil(LEVELS * jnp.log2(peak)), LOWEST)
    codes = jnp.round(value * (PEAK * jnp.exp2(level * (-1.0 / LEVELS))))
    return codes.astype(jnp.int32).astype(jnp.int16), level


def step_of(level):
    return jnp.exp2(level * (1.0 / LEVELS)) * (1.0 / PEAK)


def as_note(level, rows):
    return jnp.broadcast_to(level, (rows, level.shape[1])).astype(jnp.int32).astype(jnp.int16)


def floats(codes):
    return codes.astype(jnp.int32).astype(F32)


def pieces_of(tiles):
    above = [(a, b) for a in range(tiles) for b in range(a + 1, tiles)]
    return above, [(a, a + 1) for a in range(0, tiles, 2)]


def places():
    down = lax.broadcasted_iota(jnp.int32, (TILE, TILE), 0)
    over = lax.broadcasted_iota(jnp.int32, (TILE, TILE), 1)
    return down, over


def put_piece(piece, value, spine=None):
    codes, level = coded(value)
    piece[:TILE, :] = codes
    line = lax.broadcasted_iota(jnp.int32, (NOTE, TILE), 0)
    note = jnp.where(line < NOTE // 2, level, 0.0)
    if spine is not None:
        peak = jnp.maximum(jnp.max(jnp.abs(spine), axis=1, keepdims=True), 1e-30)
        level = jnp.maximum(jnp.ceil(LEVELS * jnp.log2(peak)), LOWEST)
        codes = jnp.round(spine * (PEAK * jnp.exp2(level * (-1.0 / LEVELS))))
        note = jnp.where(line < NOTE // 2, note, jnp.where(line < 3 * NOTE // 4, codes, level))
    piece[TILE:, :] = note.astype(jnp.int32).astype(jnp.int16)


def put_pieces(matrix, tile_of, tiles, after):
    above, paired = pieces_of(tiles)
    down, over = places()
    for index, (a, b) in enumerate(above):
        put_piece(matrix.at[index], tile_of(a, b))
        after(index)
    for index, (a, b) in enumerate(paired, len(above)):
        first = tile_of(a, a)
        spine = jnp.sum(jnp.where(down == over, first, 0.0), axis=0, keepdims=True)
        put_piece(matrix.at[index], jnp.where(down < over, first, tile_of(b, b)), spine)
        after(index)


def piece_value(piece):
    level = floats(piece[TILE:, :])[:1, :]
    return floats(piece[:TILE, :]) * step_of(level)


def diagonal_tiles(piece):
    value = piece_value(piece)
    note = floats(piece[TILE:, :])
    spine = note[NOTE // 2 : NOTE // 2 + 1, :] * step_of(note[NOTE - 1 :, :])
    down, over = places()
    across = value.T
    first = jnp.where(down < over, value, jnp.where(down == over, spine, across))
    return first, jnp.where(down < over, across, value)


def wide_coded(piece, tile, value):
    rows = value.shape[0]
    peak = jnp.maximum(jnp.max(jnp.abs(value), axis=0, keepdims=True), 1e-30)
    level = jnp.ceil(jnp.log2(peak))
    codes = jnp.round(value * jnp.exp2(WIDE - level)).astype(jnp.int32)
    first = tile * (rows + rows // 2)
    piece[first : first + rows, :] = (codes >> 8).astype(jnp.int16)
    low = codes & (BYTE - 1)
    low = low[: rows // 2, :] + (low[rows // 2 :, :] << 8) - HALFWAY
    piece[first + rows : first + rows + rows // 2, :] = low.astype(jnp.int16)
    return level


def wide_decoded(piece, tile, rows, tiles):
    first = tile * (rows + rows // 2)
    note = tiles * (rows + rows // 2)
    line = tile * (NOTE // tiles)
    level = floats(piece[note : note + NOTE, :])[line : line + 1, :]
    low = piece[first + rows : first + rows + rows // 2, :].astype(jnp.int32) + HALFWAY
    low = jnp.concatenate([low & (BYTE - 1), low >> 8], axis=0)
    codes = (piece[first : first + rows, :].astype(jnp.int32) << 8) + low
    return codes.astype(F32) * jnp.exp2(level - WIDE)


def dot(former, latter):
    return jnp.dot(former, latter, preferred_element_type=F32)


def dot_transposed(former, latter):
    return lax.dot_general(former, latter, (((1,), (1,)), ((), ())), preferred_element_type=F32)


def diagonal(rows, first, columns):
    across = lax.broadcasted_iota(jnp.int32, (rows, columns), 1)
    return lax.broadcasted_iota(jnp.int32, (rows, columns), 0) + first == across


class Pair:
    def __init__(self, high, low):
        self.high, self.low = high, low

    def put(self, rows, columns, value):
        self.high[rows, columns], self.low[rows, columns] = split(value)

    def put_symmetric(self, halves, corner, first, last):
        top, bottom = halves
        high, low = split(corner)
        self.high[top, bottom], self.low[top, bottom] = high, low
        self.high[bottom, top], self.low[bottom, top] = high.T, low.T
        self.put(top, top, first)
        self.put(bottom, bottom, last)


def product(former, latter, rows, columns, multiply=dot):
    def side(ref):
        return ref[:, columns] if multiply is dot else ref[columns, :]

    return multiply(former.high[rows, :], side(latter.high)) + (
        multiply(former.high[rows, :], side(latter.low))
        + multiply(former.low[rows, :], side(latter.high))
    )


def symmetric_product(former, latter, halves, multiply=dot):
    top, bottom = halves
    return [
        product(former, latter, rows, columns, multiply)
        for rows, columns in ((top, bottom), (top, top), (bottom, bottom))
    ]


def kernel(
    extent,
    blocks,
    experts,
    owner_list,
    grads,
    stats,
    owner_terms,
    codes_out,
    owner_ref,
    own,
    part,
    total,
    sent,
    received,
    previous,
    stat_codes,
    gathered,
    chosen,
    home_stat,
    term_codes,
    terms_in,
    terms_out,
    matrix,
    halves,
    band_codes,
    load_sem,
    stat_sem,
    owner_sem,
    ready_sem,
    open_sem,
    core_send,
    core_recv,
    ring_send,
    ring_recv,
    plane_send,
    plane_recv,
    home_send,
    home_recv,
    back_send,
    back_recv,
    spread_send,
    spread_recv,
    band_send,
    band_recv,
    out_sem,
    own_sem,
):
    dp = lax.axis_index("dp")
    spot = lax.axis_index("expert")
    x, core = dp // CORES, dp % CORES
    twin = x * CORES + 1 - core
    right = lax.rem(x + 1, RING) * CORES + core
    left = lax.rem(x + RING - 1, RING) * CORES + core
    slot, band = lax.rem(spot, 2), spot // 2
    served = 2 * dp + slot
    own_band = band == dp
    tiles = extent // TILE
    above, paired = pieces_of(tiles)
    half = extent // 2

    def block_of(turn, which):
        return lax.rem(x + turn, RING) * CORES + which

    loads = {}
    for turn in (2, 1, 3, 0):
        loads[turn] = pltpu.make_async_copy(
            grads.at[block_of(turn, core)], own.at[turn], load_sem.at[turn]
        )
        loads[turn].start()
    stat_load = pltpu.make_async_copy(stats, previous, stat_sem)
    stat_load.start()
    owner_load = pltpu.make_async_copy(owner_list, owner_ref, owner_sem)
    owner_load.start()

    barrier = pltpu.get_barrier_semaphore()
    gate = dp == 0

    def tell(semaphore, to_dp, to_expert):
        pl.semaphore_signal(
            semaphore, inc=1, device_id={"dp": to_dp, "expert": to_expert}, device_id_type=MESH
        )

    @pl.loop(1, blocks)
    def _(step):
        other = lax.rem(dp + step, blocks)

        @pl.when(other != 0)
        def _():
            tell(barrier, other, spot)

    def tile_at(index):
        return slice(index * TILE, (index + 1) * TILE)

    stat_load.wait()
    for where in range(2):
        put_pieces(
            stat_codes.at[where],
            lambda a, b, where=where: previous[where, tile_at(a), tile_at(b)],
            tiles,
            lambda index: None,
        )

    @pl.when(jnp.logical_not(gate))
    def _():
        pl.semaphore_wait(barrier, blocks - 1)
        tell(ready_sem, 0, spot)

    @pl.when(gate)
    def _():
        pl.semaphore_wait(ready_sem, blocks - 1)

        @pl.loop(1, experts)
        def _(step):
            tell(barrier, 0, lax.rem(spot + step, experts))

    crossing = {}
    for turn in (2, 1, 3, 0):
        crossing[turn] = remote(
            grads.at[block_of(turn, 1 - core)],
            part.at[turn],
            core_send.at[turn],
            core_recv.at[turn],
            twin,
            spot,
        )
        crossing[turn].start()

    def pair_sum(turn, rows, columns):
        return own[turn, rows, columns].astype(F32) + part[turn, rows, columns].astype(F32)

    top, bottom = pl.ds(0, half), pl.ds(half, half)
    line = lax.broadcasted_iota(jnp.int32, (NOTE, TILE), 0) // (NOTE // tiles)

    def ring(index, to):
        return remote(
            sent.at[index], received.at[index], ring_send.at[index], ring_recv.at[index], to, spot
        )

    def pass_on(index, to, turn, rows, arrived=None):
        note = jnp.zeros((NOTE, TILE), F32)
        for tile in range(tiles):
            value = pair_sum(turn, rows, pl.ds(tile * TILE, TILE))
            if arrived is not None:
                value = value + wide_decoded(received.at[arrived], tile, half, tiles)
            note = jnp.where(line == tile, wide_coded(sent.at[index], tile, value), note)
        sent[index, tiles * (half + half // 2) :, :] = as_note(note, NOTE)
        copy = ring(index, to)
        copy.start()
        return copy

    loads[2].wait()
    crossing[2].wait_recv()
    far_right = pass_on(0, right, 2, top)
    far_left = pass_on(1, left, 2, bottom)
    def to_plane(other):
        return remote(
            stat_codes.at[lax.rem(other, 2), other // 2],
            gathered.at[spot],
            plane_send.at[other],
            plane_recv.at[spot],
            dp,
            other,
        )

    def from_plane(other):
        return remote(
            stat_codes.at[0, 0], gathered.at[other], plane_send.at[other], plane_recv.at[other], dp, other
        )

    @pl.when(gate)
    def _():
        pl.semaphore_wait(barrier, experts - 1)

        @pl.loop(1, blocks)
        def _(step):
            tell(open_sem, step, spot)

    @pl.when(jnp.logical_not(gate))
    def _():
        pl.semaphore_wait(open_sem, 1)

    @pl.loop(1, experts)
    def _(step):
        to_plane(lax.rem(spot + step, experts)).start()

    gathered[spot] = stat_codes[slot, band]

    loads[1].wait()
    crossing[1].wait_recv()
    direct_right = pass_on(2, right, 1, bottom)
    loads[3].wait()
    crossing[3].wait_recv()
    direct_left = pass_on(3, left, 3, top)


    loads[0].wait()
    crossing[0].wait_recv()
    for rows in (top, bottom):
        total[rows, :] = pair_sum(0, rows, pl.ds(0, extent))

    far_right.wait_recv()
    mixed_right = pass_on(4, right, 1, top, 0)
    far_left.wait_recv()
    mixed_left = pass_on(5, left, 3, bottom, 1)

    @pl.loop(1, experts)
    def _(step):
        from_plane(lax.rem(spot + step, experts)).wait_recv()

    def to_home(index):
        return remote(
            chosen.at[index],
            home_stat.at[band],
            home_send.at[index],
            home_recv.at[band],
            index,
            served,
        )

    def from_home(index):
        return remote(
            chosen.at[index],
            home_stat.at[index],
            home_send.at[index],
            home_recv.at[index],
            band,
            2 * index + slot,
        )

    owner_load.wait()
    for index in range(blocks):
        mine = jnp.logical_and(own_band, dp == index)
        chosen[index] = gathered[owner_ref[served * blocks + index]]

        @pl.when(jnp.logical_not(mine))
        def _(index=index):
            to_home(index).start()

        @pl.when(mine)
        def _(index=index):
            home_stat[index] = chosen[index]

    for copy, index, rows in (
        (direct_left, 3, top),
        (direct_right, 2, bottom),
        (mixed_right, 4, top),
        (mixed_left, 5, bottom),
    ):
        copy.wait_recv()
        for tile in range(tiles):
            columns = pl.ds(tile * TILE, TILE)
            total[rows, columns] = total[rows, columns] + wide_decoded(
                received.at[index], tile, half, tiles
            )

    grad, current, factor, result, square = (
        Pair(halves.at[2 * index], halves.at[2 * index + 1]) for index in range(5)
    )
    strips = [top, bottom]
    whole = pl.ds(0, extent)
    for rows in strips:
        grad.put(rows, whole, total[rows, :])
    corner, first, last = symmetric_product(grad, grad, strips, dot_transposed)
    matrix[top, bottom] = corner
    matrix[top, top] = first
    matrix[bottom, bottom] = last
    def to_server(index):
        return remote(
            term_codes.at[index],
            terms_in.at[dp],
            back_send.at[index],
            back_recv.at[dp],
            band,
            2 * index + slot,
        )

    def from_server(index):
        return remote(
            term_codes.at[index],
            terms_in.at[index],
            back_send.at[index],
            back_recv.at[index],
            index,
            served,
        )

    def send_term(index):
        mine = jnp.logical_and(own_band, dp == index)

        @pl.when(jnp.logical_not(mine))
        def _():
            to_server(index).start()

        @pl.when(mine)
        def _():
            terms_in[index] = term_codes[index]

    put_pieces(term_codes, lambda a, b: matrix[tile_at(a), tile_at(b)], tiles, send_term)

    @pl.loop(0, blocks)
    def _(index):
        @pl.when(jnp.logical_not(jnp.logical_and(own_band, index == dp)))
        def _():
            from_home(index).wait_recv()

    squares = jnp.zeros((1, 1), F32)
    damping = jnp.where(diagonal(TILE, 0, TILE), F32(EPSILON), F32(0.0))
    for index, (a, b) in enumerate(above):
        value = DECAY * piece_value(home_stat.at[index]) + GAIN / extent * matrix[tile_at(a), tile_at(b)]
        matrix[tile_at(a), tile_at(b)] = value
        if a // (tiles // 2) == b // (tiles // 2):
            matrix[tile_at(b), tile_at(a)] = value.T
        squares = squares + 2.0 * jnp.sum(value * value, keepdims=True)
    for index, pair in enumerate(paired, len(above)):
        for a, value in zip(pair, diagonal_tiles(home_stat.at[index])):
            value = DECAY * value + GAIN / extent * matrix[tile_at(a), tile_at(a)] + damping
            matrix[tile_at(a), tile_at(a)] = value
            squares = squares + jnp.sum(value * value, keepdims=True)

    scaling = 2.5 * lax.rsqrt(squares)
    start = jnp.sqrt(jnp.sqrt(scaling))

    def factors_of(corner, first, last):
        identity = diagonal(half, 0, half)
        return [-0.25 * corner] + [
            jnp.where(identity, 1.25 - 0.25 * block, -0.25 * block) for block in (first, last)
        ]

    scaled = [
        matrix[rows, columns] * scaling
        for rows, columns in ((top, bottom), (top, top), (bottom, bottom))
    ]
    current.put_symmetric(strips, *scaled)
    scaled = factors_of(*scaled)
    factor.put_symmetric(strips, *scaled)
    result.put_symmetric(strips, *[start * block for block in scaled])

    keep_term = pltpu.make_async_copy(terms_out.at[spot], owner_terms.at[slot, band], own_sem)

    def spread_terms():
        @pl.loop(0, blocks)
        def _(index):
            @pl.when(jnp.logical_not(jnp.logical_and(own_band, index == dp)))
            def _():
                from_server(index).wait_recv()

        terms_in[blocks] = jnp.zeros(terms_in.shape[1:], jnp.int16)
        owners = [owner_ref[served * blocks + index] for index in range(blocks)]

        def spread_to(owner):
            at = jnp.int32(blocks)
            for index in range(blocks):
                at = jnp.where(owners[index] == owner, index, at)
            terms_out[owner] = terms_in[at]

        @pl.loop(1, experts)
        def _(step):
            other = lax.rem(spot + step, experts)
            spread_to(other)
            to_owner(other).start()

        spread_to(spot)
        keep_term.start()

    def to_owner(other):
        return remote(
            terms_out.at[other],
            owner_terms.at[slot, band],
            spread_send.at[other],
            spread_recv.at[spot],
            dp,
            other,
        )

    def from_owner(other):
        return remote(
            terms_out.at[other],
            owner_terms.at[lax.rem(other, 2), other // 2],
            spread_send.at[other],
            spread_recv.at[other],
            dp,
            other,
        )

    for repeat in range(ITERS - 1):
        squared = symmetric_product(factor, factor, strips)
        if repeat > 0:
            advanced = symmetric_product(result, factor, strips)
        square.put_symmetric(strips, *squared)
        fourth = symmetric_product(square, square, strips)
        if repeat > 0:
            result.put_symmetric(strips, *advanced)
        factor.put_symmetric(strips, *fourth)
        following = symmetric_product(factor, current, strips)
        current.put_symmetric(strips, *following)
        factor.put_symmetric(strips, *factors_of(*following))
        if repeat == 3:
            spread_terms()
    result.put_symmetric(strips, *symmetric_product(result, factor, strips))

    width = extent // blocks
    inner = tiles * width

    def to_replica(index):
        return remote(
            band_codes.at[index],
            codes_out.at[dp],
            band_send.at[index],
            band_recv.at[dp],
            index,
            spot,
        )

    def from_replica(index):
        return remote(
            band_codes.at[index],
            codes_out.at[index],
            band_send.at[index],
            band_recv.at[index],
            index,
            spot,
        )

    keep = pltpu.make_async_copy(band_codes.at[dp], codes_out.at[dp], out_sem)
    for rows in strips:
        value = product(result, grad, rows, whole)
        for index in range(rows.start // width, (rows.start + rows.size) // width):
            first = index * width - rows.start
            note = jnp.zeros((NOTE, TILE), F32)
            for tile in range(tiles):
                codes, level = coded(value[first : first + width, tile * TILE : (tile + 1) * TILE])
                band_codes[index, tile * width : (tile + 1) * width, :] = codes
                note = jnp.where(line == tile, level, note)
            band_codes[index, inner:, :] = as_note(note, NOTE)

            @pl.when(index != dp)
            def _():
                to_replica(index).start()

            @pl.when(index == dp)
            def _():
                keep.start()

    @pl.loop(1, experts)
    def _(step):
        from_owner(lax.rem(spot + step, experts)).wait_recv()

    for copy in crossing.values():
        copy.wait_send()
    for copy in (far_right, far_left, direct_right, direct_left, mixed_right, mixed_left):
        copy.wait_send()

    @pl.loop(1, experts)
    def _(step):
        other = lax.rem(spot + step, experts)
        to_plane(other).wait_send()
        to_owner(other).wait_send()

    @pl.loop(0, blocks)
    def _(index):
        @pl.when(jnp.logical_not(jnp.logical_and(own_band, index == dp)))
        def _():
            to_home(index).wait_send()
            to_server(index).wait_send()

    @pl.loop(1, blocks)
    def _(step):
        other = lax.rem(dp + step, blocks)
        to_replica(other).wait_send()
        from_replica(other).wait_recv()

    keep.wait()
    keep_term.wait()


def finish(
    codes,
    terms,
    stats,
    fresh_out,
    precond_out,
    taken,
    taken_terms,
    previous,
    precond,
    load_sem,
    store_sem,
):
    load_terms = pltpu.make_async_copy(terms, taken_terms, load_sem.at[3])
    load_terms.start()
    loads = [
        pltpu.make_async_copy(stats.at[where], previous.at[where], load_sem.at[where])
        for where in range(2)
    ]
    loads[0].start()
    load_codes = pltpu.make_async_copy(codes, taken, load_sem.at[2])
    load_codes.start()
    loads[1].start()
    blocks, width, extent = precond.shape
    tiles = extent // TILE
    inner = tiles * width
    above, paired = pieces_of(tiles)
    stores = []

    def store(src, dst, index):
        stores.append(pltpu.make_async_copy(src, dst, store_sem.at[index]))
        stores[-1].start()

    load_terms.wait()
    for part in range(2):
        loads[part].wait()

        def add(a, b, value, part=part):
            down, over = pl.ds(a * TILE, TILE), pl.ds(b * TILE, TILE)
            previous[part, down, over] = DECAY * previous[part, down, over] + GAIN / extent * value

        for index, (a, b) in enumerate(above):
            value = piece_value(taken_terms.at[part, index])
            add(a, b, value)
            add(b, a, value.T)
        for index, pair in enumerate(paired, len(above)):
            for a, value in zip(pair, diagonal_tiles(taken_terms.at[part, index])):
                add(a, a, value)
        store(previous.at[part], fresh_out.at[part], part)
        if part == 0:
            load_codes.wait()
        for index in range(part * blocks // 2, (part + 1) * blocks // 2):
            levels = floats(taken[index, inner:, :])
            for tile in range(tiles):
                line = tile * (NOTE // tiles)
                precond[index, :, tile * TILE : (tile + 1) * TILE] = floats(
                    taken[index, tile * width : (tile + 1) * width, :]
                ) * step_of(levels[line : line + 1, :])
        here = pl.ds(part * blocks // 2, blocks // 2)
        store(precond.at[here], precond_out.at[here], 2 + part)
    for copy in stores:
        copy.wait()


def per_device(grad_parts, stat_owned, owner_list):
    experts = lax.axis_size("expert")
    blocks = lax.axis_size("dp")
    partials, previous = grad_parts[0], stat_owned[0]
    extent = partials.shape[1]
    tiles = extent // TILE
    half = extent // 2
    dma = pltpu.SemaphoreType.DMA
    square = (extent, extent)
    width = extent // blocks
    inner = tiles * width + NOTE
    piece = (TILE + NOTE, TILE)
    message = tiles * (half + half // 2) + NOTE
    terms, codes = pl.pallas_call(
        functools.partial(kernel, extent, blocks, experts),
        out_shape=[
            jax.ShapeDtypeStruct((2, blocks, *piece), jnp.int16),
            jax.ShapeDtypeStruct((blocks, inner, TILE), jnp.int16),
        ],
        in_specs=[pl.BlockSpec(memory_space=pl.ANY)] * 3,
        out_specs=[pl.BlockSpec(memory_space=pl.ANY)] * 2,
        scratch_shapes=[
            pltpu.SMEM(owner_list.shape, jnp.int32),
            pltpu.VMEM((RING, *square), BF16),
            pltpu.VMEM((RING, *square), BF16),
            pltpu.VMEM(square, F32),
            pltpu.VMEM((6, message, TILE), jnp.int16),
            pltpu.VMEM((6, message, TILE), jnp.int16),
            pltpu.VMEM((2, *square), F32),
            pltpu.VMEM((2, blocks, *piece), jnp.int16),
            pltpu.VMEM((experts, *piece), jnp.int16),
            pltpu.VMEM((blocks, *piece), jnp.int16),
            pltpu.VMEM((blocks, *piece), jnp.int16),
            pltpu.VMEM((blocks, *piece), jnp.int16),
            pltpu.VMEM((blocks + 1, *piece), jnp.int16),
            pltpu.VMEM((experts, *piece), jnp.int16),
            pltpu.VMEM(square, F32),
            pltpu.VMEM((10, *square), BF16),
            pltpu.VMEM((blocks, inner, TILE), jnp.int16),
            dma((RING,)),
            dma(()),
            dma(()),
            pltpu.SemaphoreType.REGULAR,
            pltpu.SemaphoreType.REGULAR,
            dma((RING,)),
            dma((RING,)),
            dma((6,)),
            dma((6,)),
            dma((experts,)),
            dma((experts,)),
            dma((blocks,)),
            dma((blocks,)),
            dma((blocks,)),
            dma((blocks,)),
            dma((experts,)),
            dma((experts,)),
            dma((blocks,)),
            dma((blocks,)),
            dma(()),
            dma(()),
        ],
        compiler_params=pltpu.CompilerParams(
            collective_id=0, has_side_effects=True, vmem_limit_bytes=60 * 2**20
        ),
    )(owner_list, partials, previous)
    fresh, precond = pl.pallas_call(
        finish,
        out_shape=[
            jax.ShapeDtypeStruct(previous.shape, F32),
            jax.ShapeDtypeStruct((blocks, width, extent), F32),
        ],
        in_specs=[pl.BlockSpec(memory_space=pl.ANY)] * 3,
        out_specs=[pl.BlockSpec(memory_space=pl.ANY)] * 2,
        scratch_shapes=[
            pltpu.VMEM(codes.shape, jnp.int16),
            pltpu.VMEM(terms.shape, jnp.int16),
            pltpu.VMEM(previous.shape, F32),
            pltpu.VMEM((blocks, width, extent), F32),
            dma((4,)),
            dma((4,)),
        ],
        compiler_params=pltpu.CompilerParams(vmem_limit_bytes=60 * 2**20),
    )(codes, terms, previous)
    return (fresh[None], precond)


def solution(mesh):
    in_specs = (P("dp", "expert", None, None), P("expert", "dp", None, None), P())
    out_specs = (P("expert", "dp", None, None), P("expert", "dp", None))
    return jax.shard_map(
        per_device, mesh=mesh, in_specs=in_specs, out_specs=out_specs, check_vma=False
    )
```
